32 devices in a mesh: grp: 2 (over y), slab: 16 (over z, x, core).
Axes of the slice: x: 2, y: 2, z: 4, core: 2. Of those that a mesh axis runs over, the one named last changes fastest.
Arguments:
- orbital_alpha: bfloat16 [2, 1536, 2560], P('grp', 'slab'), may hold values from -0.75 to 0.75
- orbital_beta: bfloat16 [2, 1536, 2560], P('grp', 'slab'), may hold values from -0.75 to 0.75
- occ_alpha: float32 [2], replicated, may hold values from -2 to -0.3
- occ_beta: float32 [2], replicated, may hold values from -2 to -0.3
- virt_alpha: float32 [1536], replicated, may hold values from 0.1 to 3
- virt_beta: float32 [1536], replicated, may hold values from 0.1 to 3
Outputs:
- grad_alpha: float32 [2, 1536, 2560], P('grp', 'slab')
- grad_beta: float32 [2, 1536, 2560], P('grp', 'slab')
The draws below stay inside these ranges and needn't reach their ends.
All inputs are finite; a program needn't handle non-finite values.
Results may differ from the reference program's by a relative error of at most 0.0013.
Values may be sent and summed in bfloat16 or wider, within the bound.
No kernel may reach another device: no remote copies, remote signals or barrier semaphores. Data moves between devices by JAX's collectives and lax.ppermute only.
A program may use at most 128 MiB of HBM per device.

```python
import jax
import jax.numpy as jnp
from jax import lax

NV = 1536
NAUX = 2560
NI = 2
NJ = 2
A_DEV = 96


def level_of(rng, extent, cuts, smallest, largest):
    def one(position, blocks):
        heights = jax.random.uniform(jax.random.fold_in(jax.random.fold_in(rng, 6), position), (blocks,), jnp.float32, smallest / len(cuts), largest / len(cuts))
        return jnp.repeat(jnp.exp(heights), extent[position] // blocks).reshape((-1,) + (1,) * (len(extent) - position - 1))

    gain = one(*cuts[0])
    for cut in cuts[1:]:
        gain = gain * one(*cut)
    return gain


def normal_values(stream_key, shape, deviation, reach, cuts=(), kind=jnp.bfloat16):
    drawn = jax.random.normal(stream_key, shape, jnp.float32) * deviation
    if len(cuts) > 0:
        drawn = level_of(stream_key, shape, cuts, -0.22, 0.18) * drawn
    return jnp.clip(drawn, min=-reach, max=reach).astype(kind)


def setup_inputs(seed: int = 0) -> dict:
    streams_of = jax.random.split(jax.random.key(seed), 7)
    orbital_alpha = normal_values(streams_of[0], (NI, NV, NAUX), (1.75 / (NI * NV) ** 0.3333), 0.75, ((0, 2), (1, 16)))
    orbital_beta = normal_values(streams_of[1], (NJ, NV, NAUX), (1.75 / (NJ * NV) ** 0.3333), 0.75, ((0, 2), (1, 16)))
    occ_alpha = jnp.clip(jax.random.uniform(streams_of[2], (NI,), jnp.float32, -2.0, -0.3), -2.0, -0.3)
    occ_beta = jnp.clip(jax.random.uniform(streams_of[3], (NJ,), jnp.float32, -2.0, -0.3), -2.0, -0.3)
    virt_alpha = jnp.clip(jax.random.uniform(streams_of[4], (NV,), jnp.float32, 0.1, 3.0), 0.1, 3.0)
    virt_beta = jnp.clip(jax.random.uniform(streams_of[5], (NV,), jnp.float32, 0.1, 3.0), 0.1, 3.0)
    return dict(orbital_alpha=orbital_alpha, orbital_beta=orbital_beta, occ_alpha=occ_alpha, occ_beta=occ_beta, virt_alpha=virt_alpha, virt_beta=virt_beta)


def reference(orbital_alpha, orbital_beta, occ_alpha, occ_beta, virt_alpha, virt_beta):
    slabs = NV // A_DEV
    beta_blocks = jnp.moveaxis(orbital_beta.reshape(NJ, slabs, A_DEV, NAUX), 1, 0)
    virt_blocks = virt_beta.reshape(slabs, A_DEV)
    alpha_wide = orbital_alpha.astype(jnp.float32)

    def one_slab(carried, pieces):
        panel_beta, virt_slab = pieces
        panel_wide = panel_beta.astype(jnp.float32)
        integrals = jnp.einsum('iaq,jbq->iajb', alpha_wide, panel_wide)
        denominator = virt_alpha[None, :, None, None] + virt_slab[None, None, None, :] - occ_alpha[:, None, None, None] - occ_beta[None, None, :, None]
        amplitudes = (-integrals / denominator).astype(jnp.bfloat16)
        amplitudes = lax.optimization_barrier(amplitudes).astype(jnp.float32)
        partial_value = jnp.einsum('iajb,jbq->iaq', amplitudes, panel_wide)
        carried = carried + partial_value
        beta_part = jnp.einsum('iajb,iaq->jbq', amplitudes, alpha_wide)
        return carried, beta_part

    start_sum = jnp.zeros((NI, NV, NAUX), jnp.float32)
    grad_alpha, stacked = lax.scan(one_slab, start_sum, (beta_blocks, virt_blocks))
    grad_beta = jnp.moveaxis(stacked, 0, 1).reshape(NJ, NV, NAUX)
    return grad_alpha, grad_beta
```

```python
import functools

import jax
import jax.numpy as jnp
from jax import lax
from jax.experimental import pallas as pl
from jax.experimental.pallas import tpu as pltpu
from jax.sharding import PartitionSpec as P

VMEM_BYTES = 44 * 1024 * 1024


def bits_of(groups, slabs):
    slab_bits = slabs.bit_length() - 1
    total = (groups * slabs).bit_length() - 1
    shared = min(slab_bits - 1, total // 2)
    alpha = list(range(shared, 0, -1))
    beta = list(range(total - 1, slab_bits - 1, -1))
    beta = list(range(slab_bits - 1, shared, -1)) + beta + [0]
    return alpha, beta


def exchange(value, bit, devices):
    return lax.ppermute(value, ("grp", "slab"), [(d, d ^ (1 << bit)) for d in range(devices)])


def gathered(own, bits, devices):
    pieces = {0: own}
    for bit in bits:
        pieces.update({m | (1 << bit): exchange(v, bit, devices) for m, v in list(pieces.items())})
    return pieces


def contract_first(n_a, n_b, width, *refs):
    a_refs, b_refs = refs[:n_a], refs[n_a:n_a + n_b]
    va, oa, vb, ob = refs[n_a + n_b:n_a + n_b + 4]
    outs = refs[n_a + n_b + 4:]
    t_ref, bcat, gb = outs[0], outs[1], outs[2:2 + n_b]
    acat, tt = outs[2 + n_b:]
    aux = acat.shape[1]
    for p in range(n_a):
        acat[p * width:(p + 1) * width, :] = a_refs[p][...]
    for p in range(n_b):
        bcat[p * width:(p + 1) * width, :] = b_refs[p][...]
    cols = n_b * width
    step = 256 if cols % 256 == 0 else width
    for c in range(0, cols, step):
        integrals = lax.dot_general(
            acat[...], bcat[c:c + step, :], (((1,), (1,)), ((), ())), preferred_element_type=jnp.float32
        )
        den = ((va[...] + vb[:, c:c + step]) - oa[...]) - ob[:, c:c + step]
        amps = (-integrals / den).astype(jnp.bfloat16)
        t_ref[:, c:c + step] = amps
        tt[c:c + step, :] = amps.T
    tile = 512 if aux % 512 == 0 else 128

    def one(k, _):
        at = pl.ds(pl.multiple_of(k * tile, tile), tile)
        acc = jnp.dot(tt[...], acat[:, at], preferred_element_type=jnp.float32)
        for p in range(n_b):
            gb[p][:, at] = acc[p * width:(p + 1) * width, :]
        return 0

    lax.fori_loop(0, aux // tile, one, 0)


def contract_second(n_a, width, t_ref, bcat, *ga):
    aux = bcat.shape[1]
    tile = 512 if aux % 512 == 0 else 128

    def one(k, _):
        at = pl.ds(pl.multiple_of(k * tile, tile), tile)
        acc = jnp.dot(t_ref[...], bcat[:, at], preferred_element_type=jnp.float32)
        for p in range(n_a):
            ga[p][:, at] = acc[p * width:(p + 1) * width, :]
        return 0

    lax.fori_loop(0, aux // tile, one, 0)


def body(orbital_alpha, orbital_beta, occ_alpha, occ_beta, virt_alpha, virt_beta):
    groups, slabs = lax.axis_size("grp"), lax.axis_size("slab")
    devices = groups * slabs
    me = lax.axis_index("grp") * slabs + lax.axis_index("slab")
    own_occ, width, aux = orbital_alpha.shape
    own_a = orbital_alpha.reshape(own_occ * width, aux)
    own_b = orbital_beta.reshape(own_occ * width, aux)
    width = own_occ * width
    alpha_bits, beta_bits = bits_of(groups, slabs)

    def energies(masks, virt, occ):
        v_parts, o_parts = [], []
        for m in masks:
            other = jnp.bitwise_xor(me, m)
            slab, grp = other % slabs, other // slabs
            v = lax.dynamic_slice_in_dim(virt, slab * (width // own_occ), width // own_occ, 0)
            o = lax.dynamic_slice_in_dim(occ, grp * own_occ, own_occ, 0)
            v_parts.append(jnp.tile(v, own_occ))
            o_parts.append(jnp.repeat(o, width // own_occ))
        return jnp.concatenate(v_parts), jnp.concatenate(o_parts)

    wide_a, wide_b = own_a.astype(jnp.float32), own_b.astype(jnp.float32)
    stats = jnp.stack([
        jnp.max(jnp.sum(wide_a * wide_a, axis=1)),
        jnp.max(jnp.sum(wide_b * wide_b, axis=1)),
        jnp.maximum(jnp.max(jnp.abs(wide_a)), jnp.max(jnp.abs(wide_b))),
    ])
    stats = jnp.broadcast_to(stats[:, None], (3, 128))
    for bit in sorted(alpha_bits + beta_bits):
        stats = jnp.maximum(stats, exchange(stats, bit, devices))
    smallest = jnp.min(virt_alpha) + jnp.min(virt_beta) - jnp.max(occ_alpha) - jnp.max(occ_beta)
    summed = slabs * groups * width
    bound = jnp.sqrt(stats[0, 0]) * jnp.sqrt(stats[1, 0]) / smallest * stats[2, 0] * summed
    scale = 32768.0 / jnp.maximum(bound, 2e-34)
    unscale = jnp.maximum(bound, 2e-34) / 32768.0

    pieces_a = gathered(own_a, alpha_bits, devices)
    pieces_b = gathered(own_b, beta_bits, devices)
    masks_a, masks_b = sorted(pieces_a), sorted(pieces_b)
    n_a, n_b = len(masks_a), len(masks_b)
    va, oa = energies(masks_a, virt_alpha, occ_alpha)
    vb, ob = energies(masks_b, virt_beta, occ_beta)
    rows, cols = n_a * width, n_b * width
    piece = jax.ShapeDtypeStruct((width, aux), jnp.float32)
    first = pl.pallas_call(
        functools.partial(contract_first, n_a, n_b, width),
        out_shape=[jax.ShapeDtypeStruct((rows, cols), jnp.bfloat16), jax.ShapeDtypeStruct((cols, aux), jnp.bfloat16)]
        + [piece] * n_b,
        scratch_shapes=[pltpu.VMEM((rows, aux), jnp.bfloat16), pltpu.VMEM((cols, rows), jnp.bfloat16)],
        compiler_params=pltpu.CompilerParams(vmem_limit_bytes=VMEM_BYTES),
        cost_estimate=pl.CostEstimate(
            flops=4 * rows * cols * aux, bytes_accessed=(rows + 2 * cols) * aux * 2 + cols * aux * 4, transcendentals=0
        ),
        name="amplitudes_and_beta",
    )(*[pieces_a[m] for m in masks_a], *[pieces_b[m] for m in masks_b], va[:, None], oa[:, None], vb[None, :], ob[None, :])
    amps, bcat = first[0], first[1]
    gb = dict(zip(masks_b, first[2:]))
    ga = dict(zip(masks_a, pl.pallas_call(
        functools.partial(contract_second, n_a, width),
        out_shape=[piece] * n_a,
        compiler_params=pltpu.CompilerParams(vmem_limit_bytes=VMEM_BYTES),
        cost_estimate=pl.CostEstimate(
            flops=2 * rows * cols * aux, bytes_accessed=cols * aux * 2 + rows * aux * 4, transcendentals=0
        ),
        name="alpha",
    )(amps, bcat)))

    def narrow(value):
        return (value * scale).astype(jnp.float16)

    def wide(value):
        return value.astype(jnp.float32) * unscale

    def scattered(parts, bits):
        for bit in bits:
            flag = 1 << bit
            kept = {}
            for m in sorted((m for m in parts if m & flag), reverse=True):
                if bit == 0:
                    arrived = exchange(parts[m], bit, devices)
                else:
                    arrived = wide(exchange(narrow(parts[m]), bit, devices))
                kept[m ^ flag] = parts[m ^ flag] + arrived
            parts = kept
        return parts[0]

    grad_beta = scattered(gb, beta_bits[::-1])
    grad_alpha = scattered(ga, alpha_bits[::-1])
    return (grad_alpha.reshape(orbital_alpha.shape), grad_beta.reshape(orbital_beta.shape))


def solution(mesh):
    in_specs = (P("grp", "slab", None), P("grp", "slab", None), P(), P(), P(), P())
    out_specs = (P("grp", "slab", None), P("grp", "slab", None))
    return jax.shard_map(body, mesh=mesh, in_specs=in_specs, out_specs=out_specs, check_vma=False)
```

```python
import functools

import jax
import jax.numpy as jnp
from jax import lax
from jax.experimental import pallas as pl
from jax.experimental.pallas import tpu as pltpu
from jax.sharding import PartitionSpec as P

MIB = 1024 * 1024
together = lax.optimization_barrier


def bits_of(groups, slabs):
    slab_bits = slabs.bit_length() - 1
    total = (groups * slabs).bit_length() - 1
    shared = min(slab_bits - 1, total // 2)
    alpha = list(range(shared, 0, -1))
    beta = list(range(total - 1, slab_bits - 1, -1))
    beta = list(range(slab_bits - 1, shared, -1)) + beta + [0]
    return alpha, beta


def exchange(value, bit, devices):
    return lax.ppermute(value, ("grp", "slab"), [(d, d ^ (1 << bit)) for d in range(devices)])


def prepare(masks_a, masks_b, slabs, per, place, occ_a, occ_b, a_ref, b_ref, va_ref, vb_ref, stats, ninv):
    width = a_ref.shape[0]
    wide_a, wide_b = a_ref[...].astype(jnp.float32), b_ref[...].astype(jnp.float32)
    norm_a = jnp.max(jnp.sum(wide_a * wide_a, axis=1, keepdims=True), axis=0, keepdims=True)
    norm_b = jnp.max(jnp.sum(wide_b * wide_b, axis=1, keepdims=True), axis=0, keepdims=True)
    largest = jnp.maximum(jnp.abs(wide_a), jnp.abs(wide_b))
    largest = jnp.max(jnp.max(largest, axis=1, keepdims=True), axis=0, keepdims=True)
    row = lax.broadcasted_iota(jnp.int32, stats.shape, 0)
    stats[...] = jnp.where(row == 0, norm_a, jnp.where(row == 1, norm_b, largest))
    me = place[0]
    parts, occs = [], []
    for m in masks_b:
        other = jnp.bitwise_xor(me, m)
        for o in range(per):
            parts.append(vb_ref[pl.ds(other % slabs, 1), :])
            occs.append(jnp.full((1, width // per), occ_b[(other // slabs) * per + o], jnp.float32))
    vb, ob = jnp.concatenate(parts, axis=1), jnp.concatenate(occs, axis=1)
    for p, m in enumerate(masks_a):
        other = jnp.bitwise_xor(me, m)
        at = pl.multiple_of((other % slabs) * (width // per), 8)
        va = jnp.concatenate([va_ref[pl.ds(at, width // per), :]] * per, axis=0)
        oa = jnp.concatenate(
            [jnp.full((width // per, 1), occ_a[(other // slabs) * per + o], jnp.float32) for o in range(per)], axis=0
        )
        ninv[p * width:(p + 1) * width, :] = -1.0 / (((va + vb) - oa) - ob)


def contract_amplitudes(n_a, n_b, width, early, *refs):
    a_refs, b_refs, ninv = refs[:n_a], refs[n_a:n_a + n_b], refs[n_a + n_b]
    t_ref, tt, acat, bcat = refs[n_a + n_b + 1:n_a + n_b + 5]
    gb = refs[n_a + n_b + 5:]
    for p in range(n_a):
        acat[p * width:(p + 1) * width, :] = a_refs[p][...]
    for p in range(n_b):
        bcat[p * width:(p + 1) * width, :] = b_refs[p][...]
    cols = n_b * width
    step = 256 if cols % 256 == 0 else width
    for c in range(0, cols, step):
        integrals = lax.dot_general(
            acat[...], bcat[c:c + step, :], (((1,), (1,)), ((), ())), preferred_element_type=jnp.float32
        )
        amps = (integrals * ninv[:, c:c + step]).astype(jnp.bfloat16)
        t_ref[:, c:c + step] = amps
        tt[c:c + step, :] = amps.T
    rows_out(width, early, tt, acat, *gb)


def rows_out(width, span, left, right, *outs):
    aux = right.shape[1]
    tile = 512 if aux % 512 == 0 else 128
    rows = left[span[0] * width:span[1] * width, :]

    def one(k, _):
        at = pl.ds(pl.multiple_of(k * tile, tile), tile)
        acc = jnp.dot(rows, right[:, at], preferred_element_type=jnp.float32)
        for p, out in enumerate(outs):
            out[:, at] = acc[p * width:(p + 1) * width, :]
        return 0

    lax.fori_loop(0, aux // tile, one, 0)


def body(orbital_alpha, orbital_beta, occ_alpha, occ_beta, virt_alpha, virt_beta):
    groups, slabs = lax.axis_size("grp"), lax.axis_size("slab")
    devices = groups * slabs
    me = lax.axis_index("grp") * slabs + lax.axis_index("slab")
    per, block, aux = orbital_alpha.shape
    width = per * block
    own_a, own_b = orbital_alpha.reshape(width, aux), orbital_beta.reshape(width, aux)
    alpha_bits, beta_bits = bits_of(groups, slabs)

    def masks(bits):
        found = [0]
        for bit in bits[::-1]:
            found = found + [m | (1 << bit) for m in found]
        return found[::-1]

    masks_a, masks_b = masks(alpha_bits), masks(beta_bits)
    n_a, n_b = len(masks_a), len(masks_b)
    rows, cols = n_a * width, n_b * width

    pieces_a, pieces_b = {0: own_a}, {0: own_b}
    first_a, first_b = alpha_bits[0], beta_bits[0]
    near_b = exchange(own_b, first_b, devices)
    near_a = exchange(own_a, first_a, devices)
    for bit in alpha_bits[1:]:
        pieces_a.update({m | (1 << bit): exchange(v, bit, devices) for m, v in list(pieces_a.items())})
    for bit in beta_bits[1:-1]:
        pieces_b.update({m | (1 << bit): exchange(v, bit, devices) for m, v in list(pieces_b.items())})

    vmem = pl.BlockSpec(memory_space=pltpu.VMEM)
    smem = pl.BlockSpec(memory_space=pltpu.SMEM)
    stats, ninv = pl.pallas_call(
        functools.partial(prepare, masks_a, masks_b, slabs, per),
        out_shape=[jax.ShapeDtypeStruct((8, 128), jnp.float32), jax.ShapeDtypeStruct((rows, cols), jnp.float32)],
        in_specs=[smem] * 3 + [vmem] * 4,
        compiler_params=pltpu.CompilerParams(vmem_limit_bytes=12 * MIB),
        name="prepare",
    )(me.reshape(1), occ_alpha, occ_beta, own_a, own_b, virt_alpha[:, None], virt_beta.reshape(slabs, block))

    for bit in sorted(alpha_bits + beta_bits):
        stats = jnp.maximum(stats, exchange(stats, bit, devices))

    near_a, near_b, stats, pieces_a, pieces_b = together((near_a, near_b, stats, pieces_a, pieces_b))
    far_a, far_b = {1 << first_a: near_a}, {1 << first_b: near_b}
    for bit in alpha_bits[1:]:
        far_a.update({m | (1 << bit): exchange(v, bit, devices) for m, v in list(far_a.items())})
    for bit in beta_bits[1:-1]:
        far_b.update({m | (1 << bit): exchange(v, bit, devices) for m, v in list(far_b.items())})
    pieces_a.update(far_a)
    pieces_b.update(far_b)
    pieces_b.update({m | 1: exchange(v, 0, devices) for m, v in list(pieces_b.items())})

    smallest = jnp.min(virt_alpha) + jnp.min(virt_beta) - jnp.max(occ_alpha) - jnp.max(occ_beta)
    bound = jnp.sqrt(stats[0, 0]) * jnp.sqrt(stats[1, 0]) / smallest * stats[2, 0] * (devices * width)
    bound = jnp.maximum(bound, 2e-34)
    scale, unscale = 32768.0 / bound, bound / 32768.0

    piece = jax.ShapeDtypeStruct((width, aux), jnp.float32)
    early = min(2, n_b)
    first = pl.pallas_call(
        functools.partial(contract_amplitudes, n_a, n_b, width, (0, early)),
        out_shape=[
            jax.ShapeDtypeStruct((rows, cols), jnp.bfloat16),
            jax.ShapeDtypeStruct((cols, rows), jnp.bfloat16),
            jax.ShapeDtypeStruct((rows, aux), jnp.bfloat16),
            jax.ShapeDtypeStruct((cols, aux), jnp.bfloat16),
        ] + [piece] * early,
        compiler_params=pltpu.CompilerParams(vmem_limit_bytes=24 * MIB),
        cost_estimate=pl.CostEstimate(
            flops=3 * rows * cols * aux, bytes_accessed=2 * (rows + cols) * aux * 2, transcendentals=0
        ),
        name="amplitudes",
    )(*[pieces_a[m] for m in masks_a], *[pieces_b[m] for m in masks_b], ninv)
    t, tt, acat, bcat = first[:4]

    def contracted(left, right, start, stop, name):
        return pl.pallas_call(
            functools.partial(rows_out, width, (start, stop)),
            out_shape=[piece] * (stop - start),
            compiler_params=pltpu.CompilerParams(vmem_limit_bytes=24 * MIB),
            cost_estimate=pl.CostEstimate(
                flops=2 * (stop - start) * width * left.shape[1] * aux,
                bytes_accessed=(stop - start) * width * aux * 4 + right.size * 2, transcendentals=0,
            ),
            name=name,
        )(left, right)

    ga = dict(zip(masks_a, contracted(t, bcat, 0, n_a, "alpha")))
    gb = dict(zip(masks_b, list(first[4:]) + list(contracted(tt, acat, early, n_b, "beta"))))

    def narrow(value):
        return (value * scale).astype(jnp.float16)

    def wide(value):
        return value.astype(jnp.float32) * unscale

    gb = {m: v + exchange(gb[m | 1], 0, devices) for m, v in gb.items() if not m & 1}

    def scattered(parts_a, parts_b, bits_a, bits_b):
        for level in range(max(len(bits_a), len(bits_b))):
            jobs = []
            for parts, bits in ((parts_b, bits_b), (parts_a, bits_a)):
                if level < len(bits):
                    flag = 1 << bits[level]
                    jobs.append((parts, bits[level], [m for m in parts if m & flag]))
            ahead = [[m for m in ms if len(ms) == 1 or m & (1 << bits)] for (_, _, ms), bits in zip(
                jobs, [b[level + 1] if level + 1 < len(b) else 31 for b in (bits_b, bits_a) if level < len(b)])]
            sent = together([[narrow(parts[m]) for m in ms] for (parts, _, _), ms in zip(jobs, ahead)])
            got = [[exchange(v, bit, devices) for v in vs] for (_, bit, _), vs in zip(jobs, sent)]
            rest = [[narrow(parts[m]) for m in ms if m not in first] for (parts, _, ms), first in zip(jobs, ahead)]
            got, rest = together((got, rest))
            late = [[exchange(v, bit, devices) for v in vs] for (_, bit, _), vs in zip(jobs, rest)]
            for (parts, bit, ms), first, arrived, later in zip(jobs, ahead, got, late):
                others = [m for m in ms if m not in first]
                for m, v in list(zip(first, arrived)) + list(zip(others, later)):
                    parts[m ^ (1 << bit)] = parts[m ^ (1 << bit)] + wide(v)
                    del parts[m]
        return parts_a[0], parts_b[0]

    grad_alpha, grad_beta = scattered(ga, gb, alpha_bits[::-1], [b for b in beta_bits[::-1] if b])
    return (grad_alpha.reshape(orbital_alpha.shape), grad_beta.reshape(orbital_beta.shape))


def solution(mesh):
    in_specs = (P("grp", "slab", None), P("grp", "slab", None), P(), P(), P(), P())
    out_specs = (P("grp", "slab", None), P("grp", "slab", None))
    return jax.shard_map(body, mesh=mesh, in_specs=in_specs, out_specs=out_specs, check_vma=False)
```

```python
import functools

import jax
import jax.numpy as jnp
from jax import lax
from jax.experimental import pallas as pl
from jax.experimental.pallas import tpu as pltpu
from jax.sharding import PartitionSpec as P

MIB = 1024 * 1024
together = lax.optimization_barrier


def bits_of(groups, slabs):
    slab_bits = slabs.bit_length() - 1
    total = (groups * slabs).bit_length() - 1
    shared = min(slab_bits - 1, total // 2)
    alpha = [slab_bits - 1] + list(range(shared - 1, 0, -1))
    beta = list(range(slab_bits - 2, shared - 1, -1)) + list(range(total - 1, slab_bits - 1, -1)) + [0]
    return alpha, beta


def exchange(value, bit, devices):
    return lax.ppermute(value, ("grp", "slab"), [(d, d ^ (1 << bit)) for d in range(devices)])


def magnitudes(a_ref, b_ref, stats):
    wide_a, wide_b = a_ref[...].astype(jnp.float32), b_ref[...].astype(jnp.float32)
    norm_a = jnp.max(jnp.sum(wide_a * wide_a, axis=1, keepdims=True), axis=0, keepdims=True)
    norm_b = jnp.max(jnp.sum(wide_b * wide_b, axis=1, keepdims=True), axis=0, keepdims=True)
    largest = jnp.maximum(jnp.abs(wide_a), jnp.abs(wide_b))
    largest = jnp.max(jnp.max(largest, axis=1, keepdims=True), axis=0, keepdims=True)
    row = lax.broadcasted_iota(jnp.int32, stats.shape, 0)
    stats[...] = jnp.where(row == 0, norm_a, jnp.where(row == 1, norm_b, largest))


def energies(masks_a, masks_b, slabs, per, place, occ_a, occ_b, va_ref, vb_ref, least, ninv):
    width = ninv.shape[0] // len(masks_a)
    me = place[0]

    def lowest(ref):
        return jnp.min(jnp.min(ref[...], axis=1, keepdims=True), axis=0, keepdims=True)

    highest_a, highest_b = occ_a[0], occ_b[0]
    for o in range(1, occ_a.shape[0]):
        highest_a = jnp.maximum(highest_a, occ_a[o])
        highest_b = jnp.maximum(highest_b, occ_b[o])
    least[...] = jnp.broadcast_to(lowest(va_ref) + lowest(vb_ref) - highest_a - highest_b, least.shape)
    parts, occs = [], []
    for m in masks_b:
        other = jnp.bitwise_xor(me, m)
        for o in range(per):
            parts.append(vb_ref[pl.ds(other % slabs, 1), :])
            occs.append(jnp.full((1, width // per), occ_b[(other // slabs) * per + o], jnp.float32))
    vb, ob = jnp.concatenate(parts, axis=1), jnp.concatenate(occs, axis=1)
    for p, m in enumerate(masks_a):
        other = jnp.bitwise_xor(me, m)
        at = pl.multiple_of((other % slabs) * (width // per), 8)
        va = jnp.concatenate([va_ref[pl.ds(at, width // per), :]] * per, axis=0)
        oa = jnp.concatenate(
            [jnp.full((width // per, 1), occ_a[(other // slabs) * per + o], jnp.float32) for o in range(per)], axis=0
        )
        ninv[p * width:(p + 1) * width, :] = -1.0 / (((va + vb) - oa) - ob)


def contract_amplitudes(n_a, n_b, width, summed, *refs):
    a_refs, b_refs = refs[:n_a], refs[n_a:n_a + n_b]
    ninv, stats, least = refs[n_a + n_b:n_a + n_b + 3]
    t_ref, tt, acat, bcat, factors = refs[n_a + n_b + 3:n_a + n_b + 8]
    early = refs[n_a + n_b + 8:]
    bound = jnp.sqrt(stats[0:1, :]) * jnp.sqrt(stats[1:2, :]) / least[0:1, :] * stats[2:3, :] * summed
    bound = jnp.maximum(bound, 2e-34)
    factors[0:1, :] = 32768.0 / bound
    factors[1:8, :] = jnp.broadcast_to(bound / 32768.0, (7, bound.shape[1]))
    for p in range(n_a):
        acat[p * width:(p + 1) * width, :] = a_refs[p][...]
    for p in range(n_b):
        bcat[p * width:(p + 1) * width, :] = b_refs[p][...]
    cols = n_b * width
    step = 256 if cols % 256 == 0 else width
    for c in range(0, cols, step):
        integrals = lax.dot_general(
            acat[...], bcat[c:c + step, :], (((1,), (1,)), ((), ())), preferred_element_type=jnp.float32
        )
        amps = (integrals * ninv[:, c:c + step]).astype(jnp.bfloat16)
        t_ref[:, c:c + step] = amps
        tt[c:c + step, :] = amps.T
    rows_out(width, 0, tt, acat, factors, *early)


def rows_out(width, start, left, right, factors, *outs):
    aux = right.shape[1]
    tile = 512 if aux % 512 == 0 else 128
    rows = left[start * width:(start + len(outs)) * width, :]

    def one(k, _):
        at = pl.ds(pl.multiple_of(k * tile, tile), tile)
        acc = jnp.dot(rows, right[:, at], preferred_element_type=jnp.float32) * factors[0:1, 0:1]
        for p, out in enumerate(outs):
            out[:, at] = acc[p * width:(p + 1) * width, :]
        return 0

    lax.fori_loop(0, aux // tile, one, 0)


def body(orbital_alpha, orbital_beta, occ_alpha, occ_beta, virt_alpha, virt_beta):
    groups, slabs = lax.axis_size("grp"), lax.axis_size("slab")
    devices = groups * slabs
    me = lax.axis_index("grp") * slabs + lax.axis_index("slab")
    per, block, aux = orbital_alpha.shape
    width = per * block
    own_a, own_b = orbital_alpha.reshape(width, aux), orbital_beta.reshape(width, aux)
    alpha_bits, beta_bits = bits_of(groups, slabs)

    def masks(bits):
        found = [0]
        for bit in bits:
            found = found + [m | (1 << bit) for m in found]
        return found[::-1]

    masks_a, masks_b = masks(alpha_bits), masks([0] + beta_bits[:-1])
    n_a, n_b = len(masks_a), len(masks_b)
    rows, cols = n_a * width, n_b * width

    vmem = pl.BlockSpec(memory_space=pltpu.VMEM)
    smem = pl.BlockSpec(memory_space=pltpu.SMEM)
    scalars = jax.ShapeDtypeStruct((8, 128), jnp.float32)
    first_a, first_b = alpha_bits[0], beta_bits[0]
    pieces_a, pieces_b = {0: own_a}, {0: own_b}
    for bit in alpha_bits[1:]:
        pieces_a.update({m | (1 << bit): exchange(v, bit, devices) for m, v in list(pieces_a.items())})
    for bit in beta_bits[1:-1]:
        pieces_b.update({m | (1 << bit): exchange(v, bit, devices) for m, v in list(pieces_b.items())})
    near_a = exchange(own_a, first_a, devices)
    near_b = exchange(own_b, first_b, devices)
    stats = pl.pallas_call(
        magnitudes, out_shape=scalars, in_specs=[vmem] * 2,
        compiler_params=pltpu.CompilerParams(vmem_limit_bytes=8 * MIB), name="magnitudes",
    )(own_a, own_b)

    order = alpha_bits[1:] + [b for b in beta_bits[1:] if b] + [first_b, first_a, 0]
    split = len(order) - 1
    for bit in order[:split]:
        stats = jnp.maximum(stats, exchange(stats, bit, devices))

    pieces_b, pieces_a, near_a, near_b, stats, virt_alpha, virt_beta = together(
        (pieces_b, pieces_a, near_a, near_b, stats, virt_alpha, virt_beta)
    )
    far_a, far_b = {1 << first_a: near_a}, {1 << first_b: near_b}
    for bit in alpha_bits[1:]:
        far_a.update({m | (1 << bit): exchange(v, bit, devices) for m, v in list(far_a.items())})
    for bit in beta_bits[1:-1]:
        far_b.update({m | (1 << bit): exchange(v, bit, devices) for m, v in list(far_b.items())})
    pieces_a.update(far_a)
    pieces_b.update(far_b)
    pieces_b.update({m | 1: exchange(v, 0, devices) for m, v in list(pieces_b.items())})

    least, ninv = pl.pallas_call(
        functools.partial(energies, masks_a, masks_b, slabs, per),
        out_shape=[scalars, jax.ShapeDtypeStruct((rows, cols), jnp.float32)],
        in_specs=[smem] * 3 + [vmem] * 2,
        compiler_params=pltpu.CompilerParams(vmem_limit_bytes=12 * MIB),
        name="energies",
    )(me.reshape(1), occ_alpha, occ_beta, virt_alpha[:, None], virt_beta.reshape(slabs, block))

    for bit in order[split:]:
        stats = jnp.maximum(stats, exchange(stats, bit, devices))

    piece = jax.ShapeDtypeStruct((width, aux), jnp.float32)
    early = max(n_b // 4, 2)
    opening = pl.pallas_call(
        functools.partial(contract_amplitudes, n_a, n_b, width, float(devices * width)),
        out_shape=[
            jax.ShapeDtypeStruct((rows, cols), jnp.bfloat16),
            jax.ShapeDtypeStruct((cols, rows), jnp.bfloat16),
            jax.ShapeDtypeStruct((rows, aux), jnp.bfloat16),
            jax.ShapeDtypeStruct((cols, aux), jnp.bfloat16),
            scalars,
        ] + [piece] * early,
        compiler_params=pltpu.CompilerParams(vmem_limit_bytes=28 * MIB),
        cost_estimate=pl.CostEstimate(
            flops=2 * rows * cols * aux, bytes_accessed=2 * (rows + cols) * aux * 2, transcendentals=0
        ),
        name="amplitudes",
    )(*[pieces_a[m] for m in masks_a], *[pieces_b[m] for m in masks_b], ninv, stats, least)
    t, tt, acat, bcat, factors = opening[:5]

    def contracted(left, right, start, names, name):
        outs = pl.pallas_call(
            functools.partial(rows_out, width, start),
            out_shape=[piece] * len(names),
            compiler_params=pltpu.CompilerParams(vmem_limit_bytes=28 * MIB),
            cost_estimate=pl.CostEstimate(
                flops=2 * len(names) * width * right.size, bytes_accessed=len(names) * width * aux * 4 + right.size * 2,
                transcendentals=0,
            ),
            name=name,
        )(left, right, factors)
        return dict(zip(names, outs))

    def narrow(parts, names):
        return [parts[m].astype(jnp.float16) for m in names]

    def passed_on(names, bits, level):
        flag = 1 << bits[level]
        gone = sum(1 << b for b in bits[:level])
        every = [m for m in names if m & flag and not m & gone]
        after = 1 << bits[level + 1] if level + 1 < len(bits) else flag
        ahead = [m for m in every if m & after]
        return ahead, [m for m in every if m not in ahead]

    def chips_sum(found):
        return {m: v + exchange(found[m | 1], 0, devices) for m, v in found.items() if not m & 1}

    bits_a, bits_b = alpha_bits[::-1], [b for b in beta_bits[::-1] if b]
    names_b = [m for m in masks_b if not m & 1]
    gb = chips_sum(dict(zip(masks_b, opening[5:])))
    ga = contracted(t, bcat, 0, masks_a, "alpha")
    for level in range(max(len(bits_a), len(bits_b))):
        jobs = [
            (parts, bits[level]) + passed_on(names, bits, level)
            for parts, names, bits in ((ga, masks_a, bits_a), (gb, names_b, bits_b)) if level < len(bits)
        ]
        sent, tt, acat = together(([narrow(parts, ahead) for parts, _, ahead, _ in jobs], tt, acat))
        got = [[exchange(v, bit, devices) for v in vs] for (_, bit, _, _), vs in zip(jobs, sent)]
        if level == 0:
            gb.update(chips_sum(contracted(tt, acat, early, masks_b[early:], "beta")))
        got, rest = together((got, [narrow(parts, others) for parts, _, _, others in jobs]))
        late = [[exchange(v, bit, devices) for v in vs] for (_, bit, _, _), vs in zip(jobs, rest)]
        for (parts, bit, ahead, others), arrived, later in zip(jobs, got, late):
            for m, v in zip(ahead + others, arrived + later):
                parts[m ^ (1 << bit)] = parts[m ^ (1 << bit)] + v.astype(jnp.float32)
    total_a, total_b = ga[0], gb[0]

    unscale = factors[1:2, 0:1]
    return ((total_a * unscale).reshape(orbital_alpha.shape), (total_b * unscale).reshape(orbital_beta.shape))


def solution(mesh):
    in_specs = (P("grp", "slab", None), P("grp", "slab", None), P(), P(), P(), P())
    out_specs = (P("grp", "slab", None), P("grp", "slab", None))
    return jax.shard_map(body, mesh=mesh, in_specs=in_specs, out_specs=out_specs, check_vma=False)
```

```python
import functools

import jax
import jax.numpy as jnp
from jax import lax
from jax.experimental import pallas as pl
from jax.experimental.pallas import tpu as pltpu
from jax.sharding import PartitionSpec as P

MIB = 1024 * 1024
together = lax.optimization_barrier


def bits_of(groups, slabs):
    slab_bits = slabs.bit_length() - 1
    total = (groups * slabs).bit_length() - 1
    shared = min(slab_bits - 1, total // 2)
    alpha = [slab_bits - 1] + list(range(shared - 1, 0, -1))
    beta = list(range(slab_bits - 2, shared - 1, -1)) + list(range(total - 1, slab_bits - 1, -1)) + [0]
    return alpha, beta


def exchange(value, bit, devices):
    return lax.ppermute(value, ("grp", "slab"), [(d, d ^ (1 << bit)) for d in range(devices)])


def energies(masks_a, masks_b, slabs, per, place, occ_a, occ_b, va_ref, vb_ref, ninv):
    width = ninv.shape[0] // len(masks_a)
    me = place[0]
    parts, occs = [], []
    for m in masks_b:
        other = jnp.bitwise_xor(me, m)
        for o in range(per):
            parts.append(vb_ref[pl.ds(other % slabs, 1), :])
            occs.append(jnp.full((1, width // per), occ_b[(other // slabs) * per + o], jnp.float32))
    vb, ob = jnp.concatenate(parts, axis=1), jnp.concatenate(occs, axis=1)
    for p, m in enumerate(masks_a):
        other = jnp.bitwise_xor(me, m)
        at = pl.multiple_of((other % slabs) * (width // per), 8)
        va = jnp.concatenate([va_ref[pl.ds(at, width // per), :]] * per, axis=0)
        oa = jnp.concatenate(
            [jnp.full((width // per, 1), occ_a[(other // slabs) * per + o], jnp.float32) for o in range(per)], axis=0
        )
        ninv[p * width:(p + 1) * width, :] = -1.0 / (((va + vb) - oa) - ob)


def magnitude(value):
    return jnp.max(jnp.max(jnp.abs(value), axis=1, keepdims=True), axis=0, keepdims=True).astype(jnp.float32)


def contract_amplitudes(n_a, n_b, early, spans, *refs):
    a_refs, b_refs, ninv = refs[:n_a], refs[n_a:n_a + n_b], refs[n_a + n_b]
    t_ref, tt, acat, bcat, scale_a, unit_a, unit_b = refs[n_a + n_b + 1:n_a + n_b + 8]
    outs = refs[n_a + n_b + 8:]
    largest = []
    for sources, joined in ((a_refs, acat), (b_refs, bcat)):
        at, top = 0, None
        for ref in sources:
            value = ref[...]
            joined[at:at + ref.shape[0], :] = value
            at += ref.shape[0]
            top = magnitude(value) if top is None else jnp.maximum(top, magnitude(value))
        largest.append(top)
    rows, cols = t_ref.shape
    step = 256 if cols % 256 == 0 else cols // 2
    top = None
    for c in range(0, cols, step):
        integrals = lax.dot_general(
            acat[...], bcat[c:c + step, :], (((1,), (1,)), ((), ())), preferred_element_type=jnp.float32
        )
        amps = integrals * ninv[:, c:c + step]
        top = magnitude(amps) if top is None else jnp.maximum(top, magnitude(amps))
        amps = amps.astype(jnp.bfloat16)
        t_ref[:, c:c + step] = amps
        tt[c:c + step, :] = amps.T
    unit = top * largest[1] * (float(cols) / 32768.0) + 1e-36
    unit_a[...] = jnp.broadcast_to(unit, unit_a.shape)
    scale_a[...] = jnp.broadcast_to(1.0 / unit, scale_a.shape)
    unit_b[...] = jnp.broadcast_to(top * largest[0] * (float(rows) / 32768.0) + 1e-36, unit_b.shape)
    rows_out(0, spans, tt, acat, *outs)


def rows_out(start, spans, left, right, *outs):
    aux = right.shape[1]
    tile = 512 if aux % 512 == 0 else 128
    rows = left[start:start + sum(spans), :]

    def one(k, _):
        at = pl.ds(pl.multiple_of(k * tile, tile), tile)
        acc = jnp.dot(rows, right[:, at], preferred_element_type=jnp.float32)
        low = 0
        for span, out in zip(spans, outs):
            out[:, at] = acc[low:low + span, :]
            low += span
        return 0

    lax.fori_loop(0, aux // tile, one, 0)


def body(orbital_alpha, orbital_beta, occ_alpha, occ_beta, virt_alpha, virt_beta):
    groups, slabs = lax.axis_size("grp"), lax.axis_size("slab")
    devices = groups * slabs
    me = lax.axis_index("grp") * slabs + lax.axis_index("slab")
    per, block, aux = orbital_alpha.shape
    width = per * block
    own_a, own_b = orbital_alpha.reshape(width, aux), orbital_beta.reshape(width, aux)
    alpha_bits, beta_bits = bits_of(groups, slabs)

    def masks(bits):
        found = [0]
        for bit in bits:
            found = found + [m | (1 << bit) for m in found]
        return found[::-1]

    masks_a, masks_b = masks(alpha_bits), masks([0] + beta_bits[:-1])
    n_a, n_b = len(masks_a), len(masks_b)
    rows, cols = n_a * width, n_b * width

    cut = [width]

    def sent_on(pieces, bits):
        for bit in bits:
            pieces = dict(pieces)
            pieces.update({m | (1 << bit): [exchange(v, bit, devices) for v in vs] for m, vs in list(pieces.items())})
        return pieces

    first_a, first_b = alpha_bits[0], beta_bits[0]
    pieces_a, pieces_b = sent_on({0: [own_a]}, alpha_bits[1:]), sent_on({0: [own_b]}, beta_bits[1:-1])
    near_a, near_b = exchange(own_a, first_a, devices), exchange(own_b, first_b, devices)
    vmem = pl.BlockSpec(memory_space=pltpu.VMEM)
    smem = pl.BlockSpec(memory_space=pltpu.SMEM)
    ninv = pl.pallas_call(
        functools.partial(energies, masks_a, masks_b, slabs, per),
        out_shape=jax.ShapeDtypeStruct((rows, cols), jnp.float32),
        in_specs=[smem] * 3 + [vmem] * 2,
        compiler_params=pltpu.CompilerParams(vmem_limit_bytes=12 * MIB),
        name="energies",
    )(me.reshape(1), occ_alpha, occ_beta, virt_alpha[:, None], virt_beta.reshape(slabs, block))
    pieces_b, pieces_a, near_a, near_b, ninv = together((pieces_b, pieces_a, near_a, near_b, ninv))
    pieces_a.update(sent_on({1 << first_a: [near_a]}, alpha_bits[1:]))
    pieces_b.update(sent_on({1 << first_b: [near_b]}, beta_bits[1:-1]))
    pieces_b = sent_on(pieces_b, [0])

    def blocks(count):
        return [jax.ShapeDtypeStruct((n, aux), jnp.float32) for n in cut * count]

    def pairs(names, outs):
        return {m: [out] for m, out in zip(names, outs)}

    early = max(n_b // 4, 2)
    list_a = [v for m in masks_a for v in pieces_a[m]]
    list_b = [v for m in masks_b for v in pieces_b[m]]
    opening = pl.pallas_call(
        functools.partial(contract_amplitudes, len(list_a), len(list_b), early, cut * early),
        out_shape=[
            jax.ShapeDtypeStruct((rows, cols), jnp.bfloat16),
            jax.ShapeDtypeStruct((cols, rows), jnp.bfloat16),
            jax.ShapeDtypeStruct((rows, aux), jnp.bfloat16),
            jax.ShapeDtypeStruct((cols, aux), jnp.bfloat16),
        ] + [jax.ShapeDtypeStruct((1, aux), jnp.float32)] * 3 + blocks(early),
        compiler_params=pltpu.CompilerParams(vmem_limit_bytes=28 * MIB),
        cost_estimate=pl.CostEstimate(
            flops=2 * rows * cols * aux, bytes_accessed=2 * (rows + cols) * aux * 2, transcendentals=0
        ),
        name="amplitudes",
    )(*list_a, *list_b, ninv)
    t, tt, acat, bcat, scale_a, unit_a, unit_b = opening[:7]

    def contracted(left, right, start, names, name):
        outs = pl.pallas_call(
            functools.partial(rows_out, start * width, cut * len(names)),
            out_shape=blocks(len(names)),
            compiler_params=pltpu.CompilerParams(vmem_limit_bytes=28 * MIB),
            cost_estimate=pl.CostEstimate(
                flops=2 * len(names) * width * right.size, bytes_accessed=len(names) * width * aux * 4 + right.size * 2,
                transcendentals=0,
            ),
            name=name,
        )(left, right)
        return pairs(names, outs)

    def narrow(value, scale):
        return (value * scale).astype(jnp.float16)

    def wide(value, unit):
        return value.astype(jnp.float32) * unit

    def passed_on(names, bits, level):
        flag = 1 << bits[level]
        gone = sum(1 << b for b in bits[:level])
        every = [m for m in names if m & flag and not m & gone]
        after = 1 << bits[level + 1] if level + 1 < len(bits) else flag
        ahead = [m for m in every if m & after]
        return ahead, [m for m in every if m not in ahead]

    def chips_sum(found):
        return {
            m: [v + exchange(w, 0, devices) for v, w in zip(vs, found[m | 1])] for m, vs in found.items() if not m & 1
        }

    bits_a, bits_b = alpha_bits[::-1], [b for b in beta_bits[::-1] if b]
    names_b = [m for m in masks_b if not m & 1]
    unit_b = unit_b + exchange(unit_b, 0, devices)
    units, scales = [unit_a, unit_b], [scale_a, 1.0 / unit_b]
    gb = chips_sum(pairs(masks_b, opening[7:]))
    ga = contracted(t, bcat, 0, masks_a, "alpha")
    for level in range(max(len(bits_a), len(bits_b))):
        jobs = [
            (which, parts, bits[level]) + passed_on(names, bits, level)
            for which, parts, names, bits in ((0, ga, masks_a, bits_a), (1, gb, names_b, bits_b)) if level < len(bits)
        ]

        def made(names_at):
            return [[narrow(job[1][m][0], scales[job[0]]) for m in job[names_at]] for job in jobs]

        def moved(values):
            return [[exchange(v, job[2], devices) for v in vs] for job, vs in zip(jobs, values)]

        def added(names_at, values):
            for job, vs in zip(jobs, values):
                for m, v in zip(job[names_at], vs):
                    job[1][m ^ (1 << job[2])][0] += wide(v, partner[job[0]])

        if level == 0:
            sent, units, tt, acat = together((made(3), units, tt, acat))
        else:
            sent = made(3)
        got = moved(sent)
        partner = {job[0]: exchange(units[job[0]], job[2], devices) for job in jobs}
        if level == 0:
            gb.update(chips_sum(contracted(tt, acat, early, masks_b[early:], "beta")))
        got, rest = together((got, made(4)))
        rest = moved(rest)
        added(3, got)
        added(4, rest)
        units = [units[w] + partner[w] if w in partner else units[w] for w in range(2)]
        scales = [1.0 / unit for unit in units]

    def whole(parts):
        return parts[0].reshape(orbital_alpha.shape)

    return whole(ga[0]), whole(gb[0])


def solution(mesh):
    in_specs = (P("grp", "slab", None), P("grp", "slab", None), P(), P(), P(), P())
    out_specs = (P("grp", "slab", None), P("grp", "slab", None))
    return jax.shard_map(body, mesh=mesh, in_specs=in_specs, out_specs=out_specs, check_vma=False)
```

```python
import functools

import jax
import jax.numpy as jnp
from jax import lax
from jax.experimental import pallas as pl
from jax.experimental.pallas import tpu as pltpu
from jax.sharding import PartitionSpec as P

MIB = 1024 * 1024
together = lax.optimization_barrier


def bits_of(groups, slabs):
    slab_bits = slabs.bit_length() - 1
    total = (groups * slabs).bit_length() - 1
    shared = min(slab_bits - 1, total // 2)
    alpha = [slab_bits - 1] + list(range(shared - 1, 0, -1))
    beta = list(range(slab_bits - 2, shared - 1, -1)) + list(range(total - 1, slab_bits - 1, -1)) + [0]
    return alpha, beta


def exchange(value, bit, devices):
    return lax.ppermute(value, ("grp", "slab"), [(d, d ^ (1 << bit)) for d in range(devices)])


def energies(masks_a, masks_b, slabs, per, place, occ_a, occ_b, va_ref, vb_ref, ninv):
    width = ninv.shape[0] // len(masks_a)
    me = place[0]
    parts, occs = [], []
    for m in masks_b:
        other = jnp.bitwise_xor(me, m)
        for o in range(per):
            parts.append(vb_ref[pl.ds(other % slabs, 1), :])
            occs.append(jnp.full((1, width // per), occ_b[(other // slabs) * per + o], jnp.float32))
    vb, ob = jnp.concatenate(parts, axis=1), jnp.concatenate(occs, axis=1)
    for p, m in enumerate(masks_a):
        other = jnp.bitwise_xor(me, m)
        at = pl.multiple_of((other % slabs) * (width // per), 8)
        va = jnp.concatenate([va_ref[pl.ds(at, width // per), :]] * per, axis=0)
        oa = jnp.concatenate(
            [jnp.full((width // per, 1), occ_a[(other // slabs) * per + o], jnp.float32) for o in range(per)], axis=0
        )
        ninv[p * width:(p + 1) * width, :] = -1.0 / (((va + vb) - oa) - ob)


def magnitude(value):
    return jnp.max(jnp.max(jnp.abs(value), axis=1, keepdims=True), axis=0, keepdims=True).astype(jnp.float32)


def contract_amplitudes(n_a, n_b, early, spans, *refs):
    a_refs, b_refs, ninv = refs[:n_a], refs[n_a:n_a + n_b], refs[n_a + n_b]
    t_ref, tt, acat, bcat, scale_a, unit_a, unit_b = refs[n_a + n_b + 1:n_a + n_b + 8]
    outs = refs[n_a + n_b + 8:]
    largest = []
    for sources, joined in ((a_refs, acat), (b_refs, bcat)):
        at, top = 0, None
        for ref in sources:
            value = ref[...]
            joined[at:at + ref.shape[0], :] = value
            at += ref.shape[0]
            top = magnitude(value) if top is None else jnp.maximum(top, magnitude(value))
        largest.append(top)
    rows, cols = t_ref.shape
    step = 256 if cols % 256 == 0 else cols // 2
    top = None
    for c in range(0, cols, step):
        integrals = lax.dot_general(
            acat[...], bcat[c:c + step, :], (((1,), (1,)), ((), ())), preferred_element_type=jnp.float32
        )
        amps = integrals * ninv[:, c:c + step]
        top = magnitude(amps) if top is None else jnp.maximum(top, magnitude(amps))
        amps = amps.astype(jnp.bfloat16)
        t_ref[:, c:c + step] = amps
        tt[c:c + step, :] = amps.T
    unit = top * largest[1] * (float(cols) / 32768.0) + 1e-36
    unit_a[...] = jnp.broadcast_to(unit[0, 0], unit_a.shape)
    scale_a[...] = jnp.broadcast_to((1.0 / unit)[0, 0], scale_a.shape)
    unit_b[...] = jnp.broadcast_to((top * largest[0] * (float(rows) / 32768.0) + 1e-36)[0, 0], unit_b.shape)
    rows_out(0, spans, tt, acat, *outs)


def rows_out(start, spans, left, right, *outs):
    aux = right.shape[1]
    tile = 512 if aux % 512 == 0 else 128
    rows = left[start:start + sum(spans), :]

    def one(k, _):
        at = pl.ds(pl.multiple_of(k * tile, tile), tile)
        acc = jnp.dot(rows, right[:, at], preferred_element_type=jnp.float32)
        low = 0
        for span, out in zip(spans, outs):
            out[:, at] = acc[low:low + span, :]
            low += span
        return 0

    lax.fori_loop(0, aux // tile, one, 0)


def body(orbital_alpha, orbital_beta, occ_alpha, occ_beta, virt_alpha, virt_beta):
    groups, slabs = lax.axis_size("grp"), lax.axis_size("slab")
    devices = groups * slabs
    me = lax.axis_index("grp") * slabs + lax.axis_index("slab")
    per, block, aux = orbital_alpha.shape
    width = per * block
    own_a, own_b = orbital_alpha.reshape(width, aux), orbital_beta.reshape(width, aux)
    alpha_bits, beta_bits = bits_of(groups, slabs)

    def masks(bits):
        found = [0]
        for bit in bits:
            found = found + [m | (1 << bit) for m in found]
        return found[::-1]

    masks_a, masks_b = masks(alpha_bits), masks([0] + beta_bits[:-1])
    n_a, n_b = len(masks_a), len(masks_b)
    rows, cols = n_a * width, n_b * width

    cut = [width]

    def sent_on(pieces, bits):
        for bit in bits:
            pieces = dict(pieces)
            pieces.update({m | (1 << bit): [exchange(v, bit, devices) for v in vs] for m, vs in list(pieces.items())})
        return pieces

    first_a, first_b = alpha_bits[0], beta_bits[0]
    pieces_a, pieces_b = sent_on({0: [own_a]}, alpha_bits[1:]), sent_on({0: [own_b]}, beta_bits[1:-1])
    near_a, near_b = exchange(own_a, first_a, devices), exchange(own_b, first_b, devices)
    vmem = pl.BlockSpec(memory_space=pltpu.VMEM)
    smem = pl.BlockSpec(memory_space=pltpu.SMEM)
    ninv = pl.pallas_call(
        functools.partial(energies, masks_a, masks_b, slabs, per),
        out_shape=jax.ShapeDtypeStruct((rows, cols), jnp.float32),
        in_specs=[smem] * 3 + [vmem] * 2,
        compiler_params=pltpu.CompilerParams(vmem_limit_bytes=6 * MIB),
        name="energies",
    )(me.reshape(1), occ_alpha, occ_beta, virt_alpha[:, None], virt_beta.reshape(slabs, block))
    pieces_b, pieces_a, near_a, near_b, ninv = together((pieces_b, pieces_a, near_a, near_b, ninv))
    pieces_a.update(sent_on({1 << first_a: [near_a]}, alpha_bits[1:]))
    pieces_b.update(sent_on({1 << first_b: [near_b]}, beta_bits[1:-1]))
    pieces_b = sent_on(pieces_b, [0])

    def blocks(count):
        return [jax.ShapeDtypeStruct((n, aux), jnp.float32) for n in cut * count]

    def pairs(names, outs):
        return {m: [out] for m, out in zip(names, outs)}

    early = max(n_b // 4, 2)
    list_a = [v for m in masks_a for v in pieces_a[m]]
    list_b = [v for m in masks_b for v in pieces_b[m]]
    opening = pl.pallas_call(
        functools.partial(contract_amplitudes, len(list_a), len(list_b), early, cut * early),
        out_shape=[
            jax.ShapeDtypeStruct((rows, cols), jnp.bfloat16),
            jax.ShapeDtypeStruct((cols, rows), jnp.bfloat16),
            jax.ShapeDtypeStruct((rows, aux), jnp.bfloat16),
            jax.ShapeDtypeStruct((cols, aux), jnp.bfloat16),
        ] + [jax.ShapeDtypeStruct((aux,), jnp.float32)] * 3 + blocks(early),
        compiler_params=pltpu.CompilerParams(vmem_limit_bytes=20 * MIB),
        cost_estimate=pl.CostEstimate(
            flops=2 * rows * cols * aux, bytes_accessed=2 * (rows + cols) * aux * 2, transcendentals=0
        ),
        name="amplitudes",
    )(*list_a, *list_b, ninv)
    t, tt, acat, bcat, scale_a, unit_a, unit_b = opening[:7]

    def contracted(left, right, start, names, name):
        outs = pl.pallas_call(
            functools.partial(rows_out, start * width, cut * len(names)),
            out_shape=blocks(len(names)),
            compiler_params=pltpu.CompilerParams(vmem_limit_bytes=14 * MIB),
            cost_estimate=pl.CostEstimate(
                flops=2 * len(names) * width * right.size, bytes_accessed=len(names) * width * aux * 4 + right.size * 2,
                transcendentals=0,
            ),
            name=name,
        )(left, right)
        return pairs(names, outs)

    def narrow(value, scale):
        return (value * scale).astype(jnp.float16)

    def wide(value, unit):
        return value.astype(jnp.float32) * unit

    def passed_on(names, bits, level):
        flag = 1 << bits[level]
        gone = sum(1 << b for b in bits[:level])
        every = [m for m in names if m & flag and not m & gone]
        after = 1 << bits[level + 1] if level + 1 < len(bits) else flag
        ahead = [m for m in every if m & after]
        return ahead, [m for m in every if m not in ahead]

    def chips_sum(found):
        return {
            m: [v + exchange(w, 0, devices) for v, w in zip(vs, found[m | 1])] for m, vs in found.items() if not m & 1
        }

    bits_a, bits_b = alpha_bits[::-1], [b for b in beta_bits[::-1] if b]
    names_b = [m for m in masks_b if not m & 1]
    unit_b = unit_b + exchange(unit_b, 0, devices)
    units, scales = [unit_a, unit_b], [scale_a, 1.0 / unit_b]
    gb = chips_sum(pairs(masks_b, opening[7:]))
    ga = contracted(t, bcat, 0, masks_a, "alpha")
    for level in range(max(len(bits_a), len(bits_b))):
        jobs = [
            (which, parts, bits[level]) + passed_on(names, bits, level)
            for which, parts, names, bits in ((0, ga, masks_a, bits_a), (1, gb, names_b, bits_b)) if level < len(bits)
        ]

        before = scales

        def made(names_at, by):
            return [[narrow(job[1][m][0], by[job[0]]) for m in job[names_at]] for job in jobs]

        def moved(values):
            return [[exchange(v, job[2], devices) for v in vs] for job, vs in zip(jobs, values)]

        def added(names_at, values):
            for job, vs in zip(jobs, values):
                for m, v in zip(job[names_at], vs):
                    job[1][m ^ (1 << job[2])][0] += wide(v, partner[job[0]])

        if level == 0:
            sent, units, tt, acat = together((made(3, before), units, tt, acat))
            coming = {job[0]: exchange(units[job[0]], job[2], devices) for job in jobs}
        else:
            sent = made(3, before)
        partner = coming
        got = moved(sent)
        if level == 0:
            gb.update(chips_sum(contracted(tt, acat, early, masks_b[early:], "beta")))
        units = [units[w] + partner[w] if w in partner else units[w] for w in range(2)]
        scales = [1.0 / unit for unit in units]
        coming = {
            w: exchange(units[w], bits[level + 1], devices)
            for w, bits in ((0, bits_a), (1, bits_b)) if level + 1 < len(bits)
        }
        got, rest, coming, scales = together((got, made(4, before), coming, scales))
        rest = moved(rest)
        added(3, got)
        added(4, rest)

    def whole(parts):
        return parts[0].reshape(orbital_alpha.shape)

    return whole(ga[0]), whole(gb[0])


def solution(mesh):
    in_specs = (P("grp", "slab", None), P("grp", "slab", None), P(), P(), P(), P())
    out_specs = (P("grp", "slab", None), P("grp", "slab", None))
    return jax.shard_map(body, mesh=mesh, in_specs=in_specs, out_specs=out_specs, check_vma=False)
```

```python
import functools

import jax
import jax.numpy as jnp
from jax import lax
from jax.experimental import pallas as pl
from jax.experimental.pallas import tpu as pltpu
from jax.sharding import PartitionSpec as P

MIB = 1024 * 1024
together = lax.optimization_barrier


def bits_of(groups, slabs):
    slab_bits = slabs.bit_length() - 1
    total = (groups * slabs).bit_length() - 1
    shared = min(slab_bits - 1, total // 2)
    alpha = [slab_bits - 1] + list(range(shared - 1, 0, -1))
    beta = list(range(slab_bits - 2, shared - 1, -1)) + list(range(total - 1, slab_bits - 1, -1)) + [0]
    return alpha, beta


def exchange(value, bit, devices):
    return lax.ppermute(value, ("grp", "slab"), [(d, d ^ (1 << bit)) for d in range(devices)])


def energies(masks_a, masks_b, slabs, per, place, occ_a, occ_b, va_ref, vb_ref, ninv):
    width = ninv.shape[0] // len(masks_a)
    me = place[0]
    parts, occs = [], []
    for m in masks_b:
        other = jnp.bitwise_xor(me, m)
        for o in range(per):
            parts.append(vb_ref[pl.ds(other % slabs, 1), :])
            occs.append(jnp.full((1, width // per), occ_b[(other // slabs) * per + o], jnp.float32))
    vb, ob = jnp.concatenate(parts, axis=1), jnp.concatenate(occs, axis=1)
    for p, m in enumerate(masks_a):
        other = jnp.bitwise_xor(me, m)
        at = pl.multiple_of((other % slabs) * (width // per), 8)
        va = jnp.concatenate([va_ref[pl.ds(at, width // per), :]] * per, axis=0)
        oa = jnp.concatenate(
            [jnp.full((width // per, 1), occ_a[(other // slabs) * per + o], jnp.float32) for o in range(per)], axis=0
        )
        ninv[p * width:(p + 1) * width, :] = -1.0 / (((va + vb) - oa) - ob)


def magnitude(value):
    return jnp.max(jnp.max(jnp.abs(value), axis=1, keepdims=True), axis=0, keepdims=True).astype(jnp.float32)


def contract_amplitudes(n_a, n_b, early, spans, *refs):
    a_refs, b_refs, ninv = refs[:n_a], refs[n_a:n_a + n_b], refs[n_a + n_b]
    t_ref, tt, acat, bcat, scale_a, scale_b, unit_a, unit_b = refs[n_a + n_b + 1:n_a + n_b + 9]
    outs = refs[n_a + n_b + 9:]
    largest = []
    for sources, joined in ((a_refs, acat), (b_refs, bcat)):
        at, top = 0, None
        for ref in sources:
            value = ref[...]
            joined[at:at + ref.shape[0], :] = value
            at += ref.shape[0]
            top = magnitude(value) if top is None else jnp.maximum(top, magnitude(value))
        largest.append(top)
    rows, cols = t_ref.shape
    step = 256 if cols % 256 == 0 else cols // 2
    top = None
    for c in range(0, cols, step):
        integrals = lax.dot_general(
            acat[...], bcat[c:c + step, :], (((1,), (1,)), ((), ())), preferred_element_type=jnp.float32
        )
        amps = integrals * ninv[:, c:c + step]
        top = magnitude(amps) if top is None else jnp.maximum(top, magnitude(amps))
        amps = amps.astype(jnp.bfloat16)
        t_ref[:, c:c + step] = amps
        tt[c:c + step, :] = amps.T
    for largest_right, count, unit, scale in (
        (largest[1], cols, unit_a, scale_a), (largest[0], rows, unit_b, scale_b)
    ):
        value = top * largest_right * (count / 32768.0) + 1e-36
        unit[...] = jnp.broadcast_to(value[0, 0], unit.shape)
        scale[...] = jnp.broadcast_to((1.0 / value)[0, 0], scale.shape)
    rows_out(0, spans, tt, acat, *outs)


def rows_out(start, spans, left, right, *outs):
    aux = right.shape[1]
    tile = 512 if aux % 512 == 0 else 128
    rows = left[start:start + sum(spans), :]

    def one(k, _):
        at = pl.ds(pl.multiple_of(k * tile, tile), tile)
        acc = jnp.dot(rows, right[:, at], preferred_element_type=jnp.float32)
        low = 0
        for span, out in zip(spans, outs):
            out[:, at] = acc[low:low + span, :]
            low += span
        return 0

    lax.fori_loop(0, aux // tile, one, 0)


def body(orbital_alpha, orbital_beta, occ_alpha, occ_beta, virt_alpha, virt_beta):
    groups, slabs = lax.axis_size("grp"), lax.axis_size("slab")
    devices = groups * slabs
    me = lax.axis_index("grp") * slabs + lax.axis_index("slab")
    per, block, aux = orbital_alpha.shape
    width = per * block
    own_a, own_b = orbital_alpha.reshape(width, aux), orbital_beta.reshape(width, aux)
    alpha_bits, beta_bits = bits_of(groups, slabs)

    def masks(bits):
        found = [0]
        for bit in bits:
            found = found + [m | (1 << bit) for m in found]
        return found[::-1]

    masks_a, masks_b = masks(alpha_bits), masks([0] + beta_bits[:-1])
    n_a, n_b = len(masks_a), len(masks_b)
    rows, cols = n_a * width, n_b * width

    cut = [width]

    def sent_on(pieces, bits):
        for bit in bits:
            pieces = dict(pieces)
            pieces.update({m | (1 << bit): [exchange(v, bit, devices) for v in vs] for m, vs in list(pieces.items())})
        return pieces

    first_a, first_b = alpha_bits[0], beta_bits[0]
    pieces_a, pieces_b = sent_on({0: [own_a]}, alpha_bits[1:]), sent_on({0: [own_b]}, beta_bits[1:-1])
    near_a, near_b = exchange(own_a, first_a, devices), exchange(own_b, first_b, devices)
    vmem = pl.BlockSpec(memory_space=pltpu.VMEM)
    smem = pl.BlockSpec(memory_space=pltpu.SMEM)
    ninv = pl.pallas_call(
        functools.partial(energies, masks_a, masks_b, slabs, per),
        out_shape=jax.ShapeDtypeStruct((rows, cols), jnp.float32),
        in_specs=[smem] * 3 + [vmem] * 2,
        compiler_params=pltpu.CompilerParams(vmem_limit_bytes=6 * MIB),
        name="energies",
    )(me.reshape(1), occ_alpha, occ_beta, virt_alpha[:, None], virt_beta.reshape(slabs, block))
    pieces_b, pieces_a, near_a, near_b, ninv = together((pieces_b, pieces_a, near_a, near_b, ninv))
    pieces_a.update(sent_on({1 << first_a: [near_a]}, alpha_bits[1:]))
    pieces_b.update(sent_on({1 << first_b: [near_b]}, beta_bits[1:-1]))
    pieces_b = sent_on(pieces_b, [0])

    def blocks(count):
        return [jax.ShapeDtypeStruct((n, aux), jnp.float32) for n in cut * count]

    def pairs(names, outs):
        return {m: [out] for m, out in zip(names, outs)}

    early = max(n_b // 4, 2)
    list_a = [v for m in masks_a for v in pieces_a[m]]
    list_b = [v for m in masks_b for v in pieces_b[m]]
    opening = pl.pallas_call(
        functools.partial(contract_amplitudes, len(list_a), len(list_b), early, cut * early),
        out_shape=[
            jax.ShapeDtypeStruct((rows, cols), jnp.bfloat16),
            jax.ShapeDtypeStruct((cols, rows), jnp.bfloat16),
            jax.ShapeDtypeStruct((rows, aux), jnp.bfloat16),
            jax.ShapeDtypeStruct((cols, aux), jnp.bfloat16),
        ] + [jax.ShapeDtypeStruct((aux,), jnp.float32)] * 4 + blocks(early),
        compiler_params=pltpu.CompilerParams(vmem_limit_bytes=20 * MIB),
        cost_estimate=pl.CostEstimate(
            flops=2 * rows * cols * aux, bytes_accessed=2 * (rows + cols) * aux * 2, transcendentals=0
        ),
        name="amplitudes",
    )(*list_a, *list_b, ninv)
    t, tt, acat, bcat, scale_a, scale_b, unit_a, unit_b = opening[:8]

    def contracted(left, right, start, names, name):
        outs = pl.pallas_call(
            functools.partial(rows_out, start * width, cut * len(names)),
            out_shape=blocks(len(names)),
            compiler_params=pltpu.CompilerParams(vmem_limit_bytes=14 * MIB),
            cost_estimate=pl.CostEstimate(
                flops=2 * len(names) * width * right.size, bytes_accessed=len(names) * width * aux * 4 + right.size * 2,
                transcendentals=0,
            ),
            name=name,
        )(left, right)
        return pairs(names, outs)

    def narrow(value, scale):
        return (value * scale).astype(jnp.float16)

    def wide(value, unit):
        return value.astype(jnp.float32) * unit

    def passed_on(names, bits, level):
        flag = 1 << bits[level]
        gone = sum(1 << b for b in bits[:level])
        every = [m for m in names if m & flag and not m & gone]
        after = 1 << bits[level + 1] if level + 1 < len(bits) else flag
        ahead = [m for m in every if m & after]
        return ahead, [m for m in every if m not in ahead]

    def chips_sum(found):
        return {
            m: [v + exchange(w, 0, devices) for v, w in zip(vs, found[m | 1])] for m, vs in found.items() if not m & 1
        }

    bits_a, bits_b = alpha_bits[::-1], [b for b in beta_bits[::-1] if b]
    names_b = [m for m in masks_b if not m & 1]
    unit_other = exchange(unit_b, 0, devices)

    def chips_sum_narrow(found):
        return {
            m: [v + wide(exchange(narrow(w, scale_b), 0, devices), unit_other) for v, w in zip(vs, found[m | 1])]
            for m, vs in found.items() if not m & 1
        }

    unit_b = unit_b + unit_other
    units, scales = [unit_a, unit_b], [scale_a, 1.0 / unit_b]
    gb = chips_sum(pairs(masks_b, opening[8:]))
    ga = contracted(t, bcat, 0, masks_a, "alpha")
    for level in range(max(len(bits_a), len(bits_b))):
        jobs = [
            (which, parts, bits[level]) + passed_on(names, bits, level)
            for which, parts, names, bits in ((0, ga, masks_a, bits_a), (1, gb, names_b, bits_b)) if level < len(bits)
        ]

        before = scales

        def made(names_at, by):
            return [[narrow(job[1][m][0], by[job[0]]) for m in job[names_at]] for job in jobs]

        def moved(values):
            return [[exchange(v, job[2], devices) for v in vs] for job, vs in zip(jobs, values)]

        def added(names_at, values):
            for job, vs in zip(jobs, values):
                for m, v in zip(job[names_at], vs):
                    job[1][m ^ (1 << job[2])][0] += wide(v, partner[job[0]])

        if level == 0:
            sent, units, tt, acat = together((made(3, before), units, tt, acat))
            coming = {job[0]: exchange(units[job[0]], job[2], devices) for job in jobs}
        else:
            sent = made(3, before)
        partner = coming
        got = moved(sent)
        if level == 0:
            gb.update(chips_sum_narrow(contracted(tt, acat, early, masks_b[early:], "beta")))
        units = [units[w] + partner[w] if w in partner else units[w] for w in range(2)]
        scales = [1.0 / unit for unit in units]
        coming = {
            w: exchange(units[w], bits[level + 1], devices)
            for w, bits in ((0, bits_a), (1, bits_b)) if level + 1 < len(bits)
        }
        rest = made(4, before)
        got, rest[0], coming, scales = together((got, rest[0], coming, scales))
        rest = moved(rest)
        added(3, got)
        added(4, rest)

    def whole(parts):
        return parts[0].reshape(orbital_alpha.shape)

    return whole(ga[0]), whole(gb[0])


def solution(mesh):
    in_specs = (P("grp", "slab", None), P("grp", "slab", None), P(), P(), P(), P())
    out_specs = (P("grp", "slab", None), P("grp", "slab", None))
    return jax.shard_map(body, mesh=mesh, in_specs=in_specs, out_specs=out_specs, check_vma=False)
```

```python
import functools

import jax
import jax.numpy as jnp
from jax import lax
from jax.experimental import pallas as pl
from jax.experimental.pallas import tpu as pltpu
from jax.sharding import PartitionSpec as P

MIB = 1024 * 1024
together = lax.optimization_barrier


def bits_of(groups, slabs):
    slab_bits = slabs.bit_length() - 1
    total = (groups * slabs).bit_length() - 1
    shared = min(slab_bits - 1, total // 2)
    alpha = [slab_bits - 1] + list(range(shared - 1, 0, -1))
    beta = list(range(slab_bits - 2, shared - 1, -1)) + list(range(total - 1, slab_bits - 1, -1)) + [0]
    return alpha, beta


def exchange(value, bit, devices):
    return lax.ppermute(value, ("grp", "slab"), [(d, d ^ (1 << bit)) for d in range(devices)])


def energies(masks_a, masks_b, slabs, per, place, occ_a, occ_b, va_ref, vb_ref, ninv):
    width = ninv.shape[0] // len(masks_a)
    me = place[0]
    parts, occs = [], []
    for m in masks_b:
        other = jnp.bitwise_xor(me, m)
        for o in range(per):
            parts.append(vb_ref[pl.ds(other % slabs, 1), :])
            occs.append(jnp.full((1, width // per), occ_b[(other // slabs) * per + o], jnp.float32))
    vb, ob = jnp.concatenate(parts, axis=1), jnp.concatenate(occs, axis=1)
    for p, m in enumerate(masks_a):
        other = jnp.bitwise_xor(me, m)
        at = pl.multiple_of((other % slabs) * (width // per), 8)
        va = jnp.concatenate([va_ref[pl.ds(at, width // per), :]] * per, axis=0)
        oa = jnp.concatenate(
            [jnp.full((width // per, 1), occ_a[(other // slabs) * per + o], jnp.float32) for o in range(per)], axis=0
        )
        ninv[p * width:(p + 1) * width, :] = -1.0 / (((va + vb) - oa) - ob)


def magnitude(value):
    return jnp.max(jnp.max(jnp.abs(value), axis=1, keepdims=True), axis=0, keepdims=True).astype(jnp.float32)


def amplitudes_of(rows, cols, acat, bcat, ninv, t_ref, tt):
    top = jnp.zeros((1, 1), jnp.float32)
    step = 256 if (cols[1] - cols[0]) % 256 == 0 else cols[1] - cols[0]
    for c in range(cols[0], cols[1], step):
        integrals = lax.dot_general(
            acat[rows[0]:rows[1], :], bcat[c:c + step, :], (((1,), (1,)), ((), ())), preferred_element_type=jnp.float32
        )
        amps = integrals * ninv[rows[0]:rows[1], c:c + step]
        top = jnp.maximum(top, magnitude(amps))
        amps = amps.astype(jnp.bfloat16)
        t_ref[rows[0]:rows[1], c:c + step] = amps
        tt[c:c + step, rows[0]:rows[1]] = amps.T
    return top


def joined(sources, places, target):
    top = jnp.zeros((1, 1), jnp.float32)
    for ref, at in zip(sources, places):
        value = ref[...]
        target[at:at + ref.shape[0], :] = value
        top = jnp.maximum(top, magnitude(value))
    return top


def begin_amplitudes(places_a, places_b, corner, *refs):
    n_a, n_b = len(places_a), len(places_b)
    a_refs, b_refs, ninv = refs[:n_a], refs[n_a:n_a + n_b], refs[n_a + n_b]
    t_ref, tt, acat, bcat, tops = refs[n_a + n_b + 1:]
    top_a, top_b = joined(a_refs, places_a, acat), joined(b_refs, places_b, bcat)
    rows, cols = t_ref.shape
    top = jnp.zeros((1, 1), jnp.float32)
    if corner[0] < rows and corner[1] < cols:
        top = amplitudes_of((corner[0], rows), (corner[1], cols), acat, bcat, ninv, t_ref, tt)
    row = lax.broadcasted_iota(jnp.int32, tops.shape, 0)
    tops[...] = jnp.where(row == 0, top, jnp.where(row == 1, top_a, top_b))


def end_amplitudes(places_a, places_b, corner, spans, *refs):
    n_a, n_b = len(places_a), len(places_b)
    a_refs, b_refs, ninv = refs[:n_a], refs[n_a:n_a + n_b], refs[n_a + n_b]
    tops = refs[n_a + n_b + 5]
    t_ref, tt, acat, bcat, scale_a, scale_b, unit_a, unit_b = refs[n_a + n_b + 6:n_a + n_b + 14]
    outs = refs[n_a + n_b + 14:]
    rows, cols = t_ref.shape
    top_a = jnp.maximum(tops[1:2, 0:1], joined(a_refs, places_a, acat))
    top_b = jnp.maximum(tops[2:3, 0:1], joined(b_refs, places_b, bcat))
    top = jnp.maximum(tops[0:1, 0:1], amplitudes_of((0, corner[0]), (0, cols), acat, bcat, ninv, t_ref, tt))
    if corner[0] < rows:
        top = jnp.maximum(top, amplitudes_of((corner[0], rows), (0, corner[1]), acat, bcat, ninv, t_ref, tt))
    for largest_right, count, unit, scale in ((top_b, cols, unit_a, scale_a), (top_a, rows, unit_b, scale_b)):
        value = top * largest_right * (count / 32768.0) + 1e-36
        unit[...] = jnp.broadcast_to(value[0, 0], unit.shape)
        scale[...] = jnp.broadcast_to((1.0 / value)[0, 0], scale.shape)
    rows_out(0, spans, tt, acat, *outs)


def rows_out(start, spans, left, right, *outs):
    aux = right.shape[1]
    tile = 512 if aux % 512 == 0 else 128
    rows = left[start:start + sum(spans), :]

    def one(k, _):
        at = pl.ds(pl.multiple_of(k * tile, tile), tile)
        acc = jnp.dot(rows, right[:, at], preferred_element_type=jnp.float32)
        low = 0
        for span, out in zip(spans, outs):
            out[:, at] = acc[low:low + span, :]
            low += span
        return 0

    lax.fori_loop(0, aux // tile, one, 0)


def body(orbital_alpha, orbital_beta, occ_alpha, occ_beta, virt_alpha, virt_beta):
    groups, slabs = lax.axis_size("grp"), lax.axis_size("slab")
    devices = groups * slabs
    me = lax.axis_index("grp") * slabs + lax.axis_index("slab")
    per, block, aux = orbital_alpha.shape
    width = per * block
    own_a, own_b = orbital_alpha.reshape(width, aux), orbital_beta.reshape(width, aux)
    alpha_bits, beta_bits = bits_of(groups, slabs)

    def masks(bits):
        found = [0]
        for bit in bits:
            found = found + [m | (1 << bit) for m in found]
        return found[::-1]

    masks_a, masks_b = masks(alpha_bits), masks([0] + beta_bits[:-1])
    n_a, n_b = len(masks_a), len(masks_b)
    rows, cols = n_a * width, n_b * width

    cut = [width]

    def sent_on(pieces, bits):
        for bit in bits:
            pieces = dict(pieces)
            pieces.update({m | (1 << bit): [exchange(v, bit, devices) for v in vs] for m, vs in list(pieces.items())})
        return pieces

    first_a, first_b = alpha_bits[0], beta_bits[0]
    pieces_a, pieces_b = sent_on({0: [own_a]}, alpha_bits[1:]), sent_on({0: [own_b]}, beta_bits[1:-1])
    near_a, near_b = exchange(own_a, first_a, devices), exchange(own_b, first_b, devices)
    vmem = pl.BlockSpec(memory_space=pltpu.VMEM)
    smem = pl.BlockSpec(memory_space=pltpu.SMEM)
    ninv = pl.pallas_call(
        functools.partial(energies, masks_a, masks_b, slabs, per),
        out_shape=jax.ShapeDtypeStruct((rows, cols), jnp.float32),
        in_specs=[smem] * 3 + [vmem] * 2,
        compiler_params=pltpu.CompilerParams(vmem_limit_bytes=6 * MIB),
        name="energies",
    )(me.reshape(1), occ_alpha, occ_beta, virt_alpha[:, None], virt_beta.reshape(slabs, block))
    pieces_b, pieces_a, near_a, near_b, ninv = together((pieces_b, pieces_a, near_a, near_b, ninv))
    pieces_a.update(sent_on({1 << first_a: [near_a]}, alpha_bits[1:]))
    pieces_b.update(sent_on({1 << first_b: [near_b]}, beta_bits[1:-1]))
    pieces_b = sent_on(pieces_b, [0])

    def blocks(count):
        return [jax.ShapeDtypeStruct((n, aux), jnp.float32) for n in cut * count]

    def pairs(names, outs):
        return {m: [out] for m, out in zip(names, outs)}

    early = max(n_b // 4, 2)

    def late_first(names, first):
        late = [m for m in names if m & (1 << first) and m & ~(1 << first) & ~1]
        return len(late) if names[:len(late)] == late else len(names)

    late_a, late_b = late_first(masks_a, first_a), late_first(masks_b, first_b)
    corner = (min(-(-late_a * width // 128) * 128, rows), min(-(-late_b * width // 256) * 256, cols))
    all_a = [(v, k * width) for k, m in enumerate(masks_a) for v in pieces_a[m]]
    all_b = [(v, k * width) for k, m in enumerate(masks_b) for v in pieces_b[m]]
    shared = [
        jax.ShapeDtypeStruct((rows, cols), jnp.bfloat16),
        jax.ShapeDtypeStruct((cols, rows), jnp.bfloat16),
        jax.ShapeDtypeStruct((rows, aux), jnp.bfloat16),
        jax.ShapeDtypeStruct((cols, aux), jnp.bfloat16),
    ]

    def estimate(part):
        return pl.CostEstimate(
            flops=2 * part * aux, bytes_accessed=2 * (rows + cols) * aux * 2, transcendentals=0
        )

    begun = pl.pallas_call(
        functools.partial(begin_amplitudes, [p for _, p in all_a[late_a:]], [p for _, p in all_b[late_b:]], corner),
        out_shape=shared + [jax.ShapeDtypeStruct((8, 128), jnp.float32)],
        compiler_params=pltpu.CompilerParams(vmem_limit_bytes=18 * MIB),
        cost_estimate=estimate((rows - corner[0]) * (cols - corner[1])),
        name="amplitudes_early",
    )(*[v for v, _ in all_a[late_a:] + all_b[late_b:]], ninv)
    count = late_a + late_b + 1
    opening = pl.pallas_call(
        functools.partial(
            end_amplitudes, [p for _, p in all_a[:late_a]], [p for _, p in all_b[:late_b]], corner, cut * early
        ),
        out_shape=shared + [jax.ShapeDtypeStruct((aux,), jnp.float32)] * 4 + blocks(early),
        input_output_aliases={count + k: k for k in range(4)},
        compiler_params=pltpu.CompilerParams(vmem_limit_bytes=24 * MIB),
        cost_estimate=estimate(rows * cols),
        name="amplitudes_late",
    )(*[v for v, _ in all_a[:late_a] + all_b[:late_b]], ninv, *begun)
    t, tt, acat, bcat, scale_a, scale_b, unit_a, unit_b = opening[:8]

    def contracted(left, right, start, names, name):
        outs = pl.pallas_call(
            functools.partial(rows_out, start * width, cut * len(names)),
            out_shape=blocks(len(names)),
            compiler_params=pltpu.CompilerParams(vmem_limit_bytes=14 * MIB),
            cost_estimate=pl.CostEstimate(
                flops=2 * len(names) * width * right.size, bytes_accessed=len(names) * width * aux * 4 + right.size * 2,
                transcendentals=0,
            ),
            name=name,
        )(left, right)
        return pairs(names, outs)

    def narrow(value, scale):
        return (value * scale).astype(jnp.float16)

    def wide(value, unit):
        return value.astype(jnp.float32) * unit

    def passed_on(names, bits, level):
        flag = 1 << bits[level]
        gone = sum(1 << b for b in bits[:level])
        every = [m for m in names if m & flag and not m & gone]
        after = 1 << bits[level + 1] if level + 1 < len(bits) else flag
        ahead = [m for m in every if m & after]
        return ahead, [m for m in every if m not in ahead]

    def chips_sum(found):
        return {
            m: [v + exchange(w, 0, devices) for v, w in zip(vs, found[m | 1])] for m, vs in found.items() if not m & 1
        }

    bits_a, bits_b = alpha_bits[::-1], [b for b in beta_bits[::-1] if b]
    names_b = [m for m in masks_b if not m & 1]
    unit_other = exchange(unit_b, 0, devices)

    def chips_sum_narrow(found):
        return {
            m: [v + wide(exchange(narrow(w, scale_b), 0, devices), unit_other) for v, w in zip(vs, found[m | 1])]
            for m, vs in found.items() if not m & 1
        }

    unit_b = unit_b + unit_other
    units, scales = [unit_a, unit_b], [scale_a, 1.0 / unit_b]
    gb = chips_sum(pairs(masks_b, opening[8:]))
    ga = contracted(t, bcat, 0, masks_a, "alpha")
    for level in range(max(len(bits_a), len(bits_b))):
        jobs = [
            (which, parts, bits[level]) + passed_on(names, bits, level)
            for which, parts, names, bits in ((0, ga, masks_a, bits_a), (1, gb, names_b, bits_b)) if level < len(bits)
        ]

        before = scales

        def made(names_at, by):
            return [[narrow(job[1][m][0], by[job[0]]) for m in job[names_at]] for job in jobs]

        def moved(values):
            return [[exchange(v, job[2], devices) for v in vs] for job, vs in zip(jobs, values)]

        def added(names_at, values):
            for job, vs in zip(jobs, values):
                for m, v in zip(job[names_at], vs):
                    job[1][m ^ (1 << job[2])][0] += wide(v, partner[job[0]])

        if level == 0:
            sent, units, tt, acat = together((made(3, before), units, tt, acat))
            coming = {job[0]: exchange(units[job[0]], job[2], devices) for job in jobs}
        else:
            sent = made(3, before)
        partner = coming
        got = moved(sent)
        if level == 0:
            gb.update(chips_sum_narrow(contracted(tt, acat, early, masks_b[early:], "beta")))
        units = [units[w] + partner[w] if w in partner else units[w] for w in range(2)]
        scales = [1.0 / unit for unit in units]
        coming = {
            w: exchange(units[w], bits[level + 1], devices)
            for w, bits in ((0, bits_a), (1, bits_b)) if level + 1 < len(bits)
        }
        rest = made(4, before)
        got, rest[0], coming, scales = together((got, rest[0], coming, scales))
        rest = moved(rest)
        added(3, got)
        added(4, rest)

    def whole(parts):
        return parts[0].reshape(orbital_alpha.shape)

    return whole(ga[0]), whole(gb[0])


def solution(mesh):
    in_specs = (P("grp", "slab", None), P("grp", "slab", None), P(), P(), P(), P())
    out_specs = (P("grp", "slab", None), P("grp", "slab", None))
    return jax.shard_map(body, mesh=mesh, in_specs=in_specs, out_specs=out_specs, check_vma=False)
```

```python
import functools

import jax
import jax.numpy as jnp
from jax import lax
from jax.experimental import pallas as pl
from jax.experimental.pallas import tpu as pltpu
from jax.sharding import PartitionSpec as P

MIB = 1024 * 1024
together = lax.optimization_barrier


def bits_of(groups, slabs):
    slab_bits = slabs.bit_length() - 1
    total = (groups * slabs).bit_length() - 1
    shared = min(slab_bits - 1, total // 2)
    alpha = [slab_bits - 1] + list(range(shared - 1, 0, -1))
    beta = list(range(slab_bits - 2, shared - 1, -1)) + list(range(total - 1, slab_bits - 1, -1)) + [0]
    return alpha, beta


def exchange(value, bit, devices):
    return lax.ppermute(value, ("grp", "slab"), [(d, d ^ (1 << bit)) for d in range(devices)])


def energies(masks_a, masks_b, slabs, per, place, occ_a, occ_b, va_ref, vb_ref, ninv):
    width = ninv.shape[0] // len(masks_a)
    me = place[0]
    parts, occs = [], []
    for m in masks_b:
        other = jnp.bitwise_xor(me, m)
        for o in range(per):
            parts.append(vb_ref[pl.ds(other % slabs, 1), :])
            occs.append(jnp.full((1, width // per), occ_b[(other // slabs) * per + o], jnp.float32))
    vb, ob = jnp.concatenate(parts, axis=1), jnp.concatenate(occs, axis=1)
    for p, m in enumerate(masks_a):
        other = jnp.bitwise_xor(me, m)
        at = pl.multiple_of((other % slabs) * (width // per), 8)
        va = jnp.concatenate([va_ref[pl.ds(at, width // per), :]] * per, axis=0)
        oa = jnp.concatenate(
            [jnp.full((width // per, 1), occ_a[(other // slabs) * per + o], jnp.float32) for o in range(per)], axis=0
        )
        ninv[p * width:(p + 1) * width, :] = -1.0 / (((va + vb) - oa) - ob)


def magnitude(value):
    return jnp.max(jnp.max(jnp.abs(value), axis=1, keepdims=True), axis=0, keepdims=True).astype(jnp.float32)


def amplitudes_of(rows, cols, acat, bcat, ninv, t_ref, tt):
    top = jnp.zeros((1, 1), jnp.float32)
    step = 256 if (cols[1] - cols[0]) % 256 == 0 else cols[1] - cols[0]
    for c in range(cols[0], cols[1], step):
        integrals = lax.dot_general(
            acat[rows[0]:rows[1], :], bcat[c:c + step, :], (((1,), (1,)), ((), ())), preferred_element_type=jnp.float32
        )
        amps = integrals * ninv[rows[0]:rows[1], c:c + step]
        top = jnp.maximum(top, magnitude(amps))
        amps = amps.astype(jnp.bfloat16)
        t_ref[rows[0]:rows[1], c:c + step] = amps
        tt[c:c + step, rows[0]:rows[1]] = amps.T
    return top


def joined(sources, places, target):
    top = jnp.zeros((1, 1), jnp.float32)
    for ref, at in zip(sources, places):
        value = ref[...]
        target[at:at + ref.shape[0], :] = value
        top = jnp.maximum(top, magnitude(value))
    return top


def begin_amplitudes(places_a, places_b, corner, *refs):
    n_a, n_b = len(places_a), len(places_b)
    a_refs, b_refs, ninv = refs[:n_a], refs[n_a:n_a + n_b], refs[n_a + n_b]
    t_ref, tt, acat, bcat, tops = refs[n_a + n_b + 1:]
    top_a, top_b = joined(a_refs, places_a, acat), joined(b_refs, places_b, bcat)
    rows, cols = t_ref.shape
    top = jnp.zeros((1, 1), jnp.float32)
    if corner[0] < rows and corner[1] < cols:
        top = amplitudes_of((corner[0], rows), (corner[1], cols), acat, bcat, ninv, t_ref, tt)
    row = lax.broadcasted_iota(jnp.int32, tops.shape, 0)
    tops[...] = jnp.where(row == 0, top, jnp.where(row == 1, top_a, top_b))


def end_amplitudes(places_a, places_b, corner, spans_a, spans_b, *refs):
    n_a, n_b = len(places_a), len(places_b)
    a_refs, b_refs, ninv = refs[:n_a], refs[n_a:n_a + n_b], refs[n_a + n_b]
    tops = refs[n_a + n_b + 5]
    t_ref, tt, acat, bcat, scale_a, scale_b, unit_a, unit_b = refs[n_a + n_b + 6:n_a + n_b + 14]
    outs = refs[n_a + n_b + 14:]
    rows, cols = t_ref.shape
    top_a = jnp.maximum(tops[1:2, 0:1], joined(a_refs, places_a, acat))
    top_b = jnp.maximum(tops[2:3, 0:1], joined(b_refs, places_b, bcat))
    top = jnp.maximum(tops[0:1, 0:1], amplitudes_of((0, corner[0]), (0, cols), acat, bcat, ninv, t_ref, tt))
    if corner[0] < rows:
        top = jnp.maximum(top, amplitudes_of((corner[0], rows), (0, corner[1]), acat, bcat, ninv, t_ref, tt))
    for largest_right, count, unit, scale in ((top_b, cols, unit_a, scale_a), (top_a, rows, unit_b, scale_b)):
        value = top * largest_right * (count / 32768.0) + 1e-36
        unit[...] = jnp.broadcast_to(value[0, 0], unit.shape)
        scale[...] = jnp.broadcast_to((1.0 / value)[0, 0], scale.shape)
    rows_out(0, spans_b, tt, acat, *outs[:len(spans_b)])
    rows_out(0, spans_a, t_ref, bcat, *outs[len(spans_b):])


def rows_out(start, spans, left, right, *outs):
    aux = right.shape[1]
    tile = 512 if aux % 512 == 0 else 128
    rows = left[start:start + sum(spans), :]

    def one(k, _):
        at = pl.ds(pl.multiple_of(k * tile, tile), tile)
        acc = jnp.dot(rows, right[:, at], preferred_element_type=jnp.float32)
        low = 0
        for span, out in zip(spans, outs):
            out[:, at] = acc[low:low + span, :]
            low += span
        return 0

    lax.fori_loop(0, aux // tile, one, 0)


def body(orbital_alpha, orbital_beta, occ_alpha, occ_beta, virt_alpha, virt_beta):
    groups, slabs = lax.axis_size("grp"), lax.axis_size("slab")
    devices = groups * slabs
    me = lax.axis_index("grp") * slabs + lax.axis_index("slab")
    per, block, aux = orbital_alpha.shape
    width = per * block
    own_a, own_b = orbital_alpha.reshape(width, aux), orbital_beta.reshape(width, aux)
    alpha_bits, beta_bits = bits_of(groups, slabs)

    def masks(bits):
        found = [0]
        for bit in bits:
            found = found + [m | (1 << bit) for m in found]
        return found[::-1]

    masks_a, masks_b = masks(alpha_bits), masks([0] + beta_bits[:-1])
    n_a, n_b = len(masks_a), len(masks_b)
    rows, cols = n_a * width, n_b * width

    cut = [width]

    def sent_on(pieces, bits):
        for bit in bits:
            pieces = dict(pieces)
            pieces.update({m | (1 << bit): [exchange(v, bit, devices) for v in vs] for m, vs in list(pieces.items())})
        return pieces

    first_a, first_b = alpha_bits[0], beta_bits[0]
    pieces_a, pieces_b = sent_on({0: [own_a]}, alpha_bits[1:]), sent_on({0: [own_b]}, beta_bits[1:-1])
    near_a, near_b = exchange(own_a, first_a, devices), exchange(own_b, first_b, devices)
    vmem = pl.BlockSpec(memory_space=pltpu.VMEM)
    smem = pl.BlockSpec(memory_space=pltpu.SMEM)
    ninv = pl.pallas_call(
        functools.partial(energies, masks_a, masks_b, slabs, per),
        out_shape=jax.ShapeDtypeStruct((rows, cols), jnp.float32),
        in_specs=[smem] * 3 + [vmem] * 2,
        compiler_params=pltpu.CompilerParams(vmem_limit_bytes=6 * MIB),
        name="energies",
    )(me.reshape(1), occ_alpha, occ_beta, virt_alpha[:, None], virt_beta.reshape(slabs, block))
    pieces_b, pieces_a, near_a, near_b, ninv = together((pieces_b, pieces_a, near_a, near_b, ninv))
    pieces_a.update(sent_on({1 << first_a: [near_a]}, alpha_bits[1:]))
    pieces_b.update(sent_on({1 << first_b: [near_b]}, beta_bits[1:-1]))
    pieces_b = sent_on(pieces_b, [0])

    def blocks(count):
        return [jax.ShapeDtypeStruct((n, aux), jnp.float32) for n in cut * count]

    def pairs(names, outs):
        return {m: [out] for m, out in zip(names, outs)}

    early_a, early_b = max(n_a // 4, 1), max(n_b // 4, 2)

    def late_first(names, first):
        late = [m for m in names if m & (1 << first) and m & ~(1 << first) & ~1]
        return len(late) if names[:len(late)] == late else len(names)

    late_a, late_b = late_first(masks_a, first_a), late_first(masks_b, first_b)
    corner = (min(-(-late_a * width // 128) * 128, rows), min(-(-late_b * width // 256) * 256, cols))
    all_a = [(v, k * width) for k, m in enumerate(masks_a) for v in pieces_a[m]]
    all_b = [(v, k * width) for k, m in enumerate(masks_b) for v in pieces_b[m]]
    shared = [
        jax.ShapeDtypeStruct((rows, cols), jnp.bfloat16),
        jax.ShapeDtypeStruct((cols, rows), jnp.bfloat16),
        jax.ShapeDtypeStruct((rows, aux), jnp.bfloat16),
        jax.ShapeDtypeStruct((cols, aux), jnp.bfloat16),
    ]

    def estimate(part):
        return pl.CostEstimate(
            flops=2 * part * aux, bytes_accessed=2 * (rows + cols) * aux * 2, transcendentals=0
        )

    begun = pl.pallas_call(
        functools.partial(begin_amplitudes, [p for _, p in all_a[late_a:]], [p for _, p in all_b[late_b:]], corner),
        out_shape=shared + [jax.ShapeDtypeStruct((8, 128), jnp.float32)],
        compiler_params=pltpu.CompilerParams(vmem_limit_bytes=18 * MIB),
        cost_estimate=estimate((rows - corner[0]) * (cols - corner[1])),
        name="amplitudes_early",
    )(*[v for v, _ in all_a[late_a:] + all_b[late_b:]], ninv)
    count = late_a + late_b + 1
    opening = pl.pallas_call(
        functools.partial(
            end_amplitudes, [p for _, p in all_a[:late_a]], [p for _, p in all_b[:late_b]], corner,
            cut * early_a, cut * early_b,
        ),
        out_shape=shared + [jax.ShapeDtypeStruct((aux,), jnp.float32)] * 4 + blocks(early_a + early_b),
        input_output_aliases={count + k: k for k in range(4)},
        compiler_params=pltpu.CompilerParams(vmem_limit_bytes=24 * MIB),
        cost_estimate=estimate(rows * cols),
        name="amplitudes_late",
    )(*[v for v, _ in all_a[:late_a] + all_b[:late_b]], ninv, *begun)
    t, tt, acat, bcat, scale_a, scale_b, unit_a, unit_b = opening[:8]

    def contracted(left, right, start, names, name):
        outs = pl.pallas_call(
            functools.partial(rows_out, start * width, cut * len(names)),
            out_shape=blocks(len(names)),
            compiler_params=pltpu.CompilerParams(vmem_limit_bytes=14 * MIB),
            cost_estimate=pl.CostEstimate(
                flops=2 * len(names) * width * right.size, bytes_accessed=len(names) * width * aux * 4 + right.size * 2,
                transcendentals=0,
            ),
            name=name,
        )(left, right)
        return pairs(names, outs)

    def narrow(value, scale):
        return (value * scale).astype(jnp.float16)

    def wide(value, unit):
        return value.astype(jnp.float32) * unit

    def passed_on(names, bits, level):
        flag = 1 << bits[level]
        gone = sum(1 << b for b in bits[:level])
        every = [m for m in names if m & flag and not m & gone]
        after = 1 << bits[level + 1] if level + 1 < len(bits) else flag
        ahead = [m for m in every if m & after]
        return ahead, [m for m in every if m not in ahead]

    bits_a, bits_b = alpha_bits[::-1], [b for b in beta_bits[::-1] if b]
    names_b = [m for m in masks_b if not m & 1]
    unit_other = exchange(unit_b, 0, devices)

    def chips_sum(found):
        return {
            m: [v + wide(exchange(narrow(w, scale_b), 0, devices), unit_other) for v, w in zip(vs, found[m | 1])]
            for m, vs in found.items() if not m & 1
        }

    unit_b = unit_b + unit_other
    units, scales = [unit_a, unit_b], [scale_a, 1.0 / unit_b]
    gb = chips_sum(pairs(masks_b, opening[8:8 + early_b]))
    ga = pairs(masks_a, opening[8 + early_b:])
    for level in range(max(len(bits_a), len(bits_b))):
        jobs = [
            (which, parts, bits[level]) + passed_on(names, bits, level)
            for which, parts, names, bits in ((0, ga, masks_a, bits_a), (1, gb, names_b, bits_b)) if level < len(bits)
        ]

        before = scales

        def made(names_at, by):
            return [[narrow(job[1][m][0], by[job[0]]) for m in job[names_at]] for job in jobs]

        def moved(values):
            return [[exchange(v, job[2], devices) for v in vs] for job, vs in zip(jobs, values)]

        def added(names_at, values):
            for job, vs in zip(jobs, values):
                for m, v in zip(job[names_at], vs):
                    job[1][m ^ (1 << job[2])][0] += wide(v, partner[job[0]])

        if level == 0:
            sent, units, t, tt, acat, bcat = together((made(3, before), units, t, tt, acat, bcat))
            coming = {job[0]: exchange(units[job[0]], job[2], devices) for job in jobs}
        else:
            sent = made(3, before)
        partner = coming
        got = moved(sent)
        if level == 0:
            gb.update(chips_sum(contracted(tt, acat, early_b, masks_b[early_b:], "beta")))
            ga.update(contracted(t, bcat, early_a, masks_a[early_a:], "alpha"))
        units = [units[w] + partner[w] if w in partner else units[w] for w in range(2)]
        scales = [1.0 / unit for unit in units]
        coming = {
            w: exchange(units[w], bits[level + 1], devices)
            for w, bits in ((0, bits_a), (1, bits_b)) if level + 1 < len(bits)
        }
        rest = made(4, before)
        got, rest[0], coming, scales = together((got, rest[0], coming, scales))
        rest = moved(rest)
        added(3, got)
        added(4, rest)

    def whole(parts):
        return parts[0].reshape(orbital_alpha.shape)

    return whole(ga[0]), whole(gb[0])


def solution(mesh):
    in_specs = (P("grp", "slab", None), P("grp", "slab", None), P(), P(), P(), P())
    out_specs = (P("grp", "slab", None), P("grp", "slab", None))
    return jax.shard_map(body, mesh=mesh, in_specs=in_specs, out_specs=out_specs, check_vma=False)
```

```python
import functools

import jax
import jax.numpy as jnp
from jax import lax
from jax.experimental import pallas as pl
from jax.experimental.pallas import tpu as pltpu
from jax.sharding import PartitionSpec as P

MIB = 1024 * 1024
together = lax.optimization_barrier


def bits_of(groups, slabs):
    slab_bits = slabs.bit_length() - 1
    total = (groups * slabs).bit_length() - 1
    shared = min(slab_bits - 1, total // 2)
    alpha = [slab_bits - 1] + list(range(shared - 1, 0, -1))
    beta = list(range(slab_bits - 2, shared - 1, -1)) + list(range(total - 1, slab_bits - 1, -1)) + [0]
    return alpha, beta


def exchange(value, bit, devices):
    return lax.ppermute(value, ("grp", "slab"), [(d, d ^ (1 << bit)) for d in range(devices)])


def energies(masks_a, masks_b, slabs, per, place, occ_a, occ_b, va_ref, vb_ref, ninv):
    width = ninv.shape[0] // len(masks_a)
    me = place[0]
    parts, occs = [], []
    for m in masks_b:
        other = jnp.bitwise_xor(me, m)
        for o in range(per):
            parts.append(vb_ref[pl.ds(other % slabs, 1), :])
            occs.append(jnp.full((1, width // per), occ_b[(other // slabs) * per + o], jnp.float32))
    vb, ob = jnp.concatenate(parts, axis=1), jnp.concatenate(occs, axis=1)
    for p, m in enumerate(masks_a):
        other = jnp.bitwise_xor(me, m)
        at = pl.multiple_of((other % slabs) * (width // per), 8)
        va = jnp.concatenate([va_ref[pl.ds(at, width // per), :]] * per, axis=0)
        oa = jnp.concatenate(
            [jnp.full((width // per, 1), occ_a[(other // slabs) * per + o], jnp.float32) for o in range(per)], axis=0
        )
        ninv[p * width:(p + 1) * width, :] = -1.0 / (((va + vb) - oa) - ob)


def magnitude(value):
    return jnp.max(jnp.max(jnp.abs(value), axis=1, keepdims=True), axis=0, keepdims=True).astype(jnp.float32)


def amplitudes_of(rows, cols, acat, bcat, ninv, t_ref, tt):
    top = jnp.zeros((1, 1), jnp.float32)
    step = 256 if (cols[1] - cols[0]) % 256 == 0 else cols[1] - cols[0]
    for c in range(cols[0], cols[1], step):
        integrals = lax.dot_general(
            acat[rows[0]:rows[1], :], bcat[c:c + step, :], (((1,), (1,)), ((), ())), preferred_element_type=jnp.float32
        )
        amps = integrals * ninv[rows[0]:rows[1], c:c + step]
        top = jnp.maximum(top, magnitude(amps))
        amps = amps.astype(jnp.bfloat16)
        t_ref[rows[0]:rows[1], c:c + step] = amps
        tt[c:c + step, rows[0]:rows[1]] = amps.T
    return top


def joined(sources, places, target):
    top = jnp.zeros((1, 1), jnp.float32)
    for ref, at in zip(sources, places):
        value = ref[...]
        target[at:at + ref.shape[0], :] = value
        top = jnp.maximum(top, magnitude(value))
    return top


def begin_amplitudes(places_a, places_b, corner, *refs):
    n_a, n_b = len(places_a), len(places_b)
    a_refs, b_refs, ninv = refs[:n_a], refs[n_a:n_a + n_b], refs[n_a + n_b]
    t_ref, tt, acat, bcat, tops = refs[n_a + n_b + 1:]
    top_a, top_b = joined(a_refs, places_a, acat), joined(b_refs, places_b, bcat)
    rows, cols = t_ref.shape
    top = jnp.zeros((1, 1), jnp.float32)
    if corner[0] < rows and corner[1] < cols:
        top = amplitudes_of((corner[0], rows), (corner[1], cols), acat, bcat, ninv, t_ref, tt)
    row = lax.broadcasted_iota(jnp.int32, tops.shape, 0)
    tops[...] = jnp.where(row == 0, top, jnp.where(row == 1, top_a, top_b))


def end_amplitudes(places_a, places_b, corner, spans, *refs):
    n_a, n_b = len(places_a), len(places_b)
    a_refs, b_refs, ninv = refs[:n_a], refs[n_a:n_a + n_b], refs[n_a + n_b]
    tops = refs[n_a + n_b + 5]
    t_ref, tt, acat, bcat, scale_a, scale_b, unit_a, unit_b = refs[n_a + n_b + 6:n_a + n_b + 14]
    outs = refs[n_a + n_b + 14:]
    rows, cols = t_ref.shape
    top_a = jnp.maximum(tops[1:2, 0:1], joined(a_refs, places_a, acat))
    top_b = jnp.maximum(tops[2:3, 0:1], joined(b_refs, places_b, bcat))
    top = jnp.maximum(tops[0:1, 0:1], amplitudes_of((0, corner[0]), (0, cols), acat, bcat, ninv, t_ref, tt))
    if corner[0] < rows:
        top = jnp.maximum(top, amplitudes_of((corner[0], rows), (0, corner[1]), acat, bcat, ninv, t_ref, tt))
    for largest_right, count, unit, scale in ((top_b, cols, unit_a, scale_a), (top_a, rows, unit_b, scale_b)):
        value = top * largest_right * (count / 32768.0) + 1e-36
        unit[...] = jnp.broadcast_to(value[0, 0], unit.shape)
        scale[...] = jnp.broadcast_to((1.0 / value)[0, 0], scale.shape)
    rows_out(0, spans, tt, acat, *outs)


def rows_out(start, spans, left, right, *outs):
    aux = right.shape[1]
    tile = 512 if aux % 512 == 0 else 128
    rows = left[start:start + sum(spans), :]

    def one(k, _):
        at = pl.ds(pl.multiple_of(k * tile, tile), tile)
        acc = jnp.dot(rows, right[:, at], preferred_element_type=jnp.float32)
        low = 0
        for span, out in zip(spans, outs):
            out[:, at] = acc[low:low + span, :]
            low += span
        return 0

    lax.fori_loop(0, aux // tile, one, 0)


def body(orbital_alpha, orbital_beta, occ_alpha, occ_beta, virt_alpha, virt_beta):
    groups, slabs = lax.axis_size("grp"), lax.axis_size("slab")
    devices = groups * slabs
    me = lax.axis_index("grp") * slabs + lax.axis_index("slab")
    per, block, aux = orbital_alpha.shape
    width = per * block
    own_a, own_b = orbital_alpha.reshape(width, aux), orbital_beta.reshape(width, aux)
    alpha_bits, beta_bits = bits_of(groups, slabs)

    def masks(bits):
        found = [0]
        for bit in bits:
            found = found + [m | (1 << bit) for m in found]
        return found[::-1]

    masks_a, masks_b = masks(alpha_bits), masks([0] + beta_bits[:-1])
    n_a, n_b = len(masks_a), len(masks_b)
    rows, cols = n_a * width, n_b * width

    cut = [width]

    def sent_on(pieces, bits):
        for bit in bits:
            pieces = dict(pieces)
            pieces.update({m | (1 << bit): [exchange(v, bit, devices) for v in vs] for m, vs in list(pieces.items())})
        return pieces

    first_a, first_b = alpha_bits[0], beta_bits[0]
    pieces_a, pieces_b = sent_on({0: [own_a]}, alpha_bits[1:]), sent_on({0: [own_b]}, beta_bits[1:-1])
    near_a, near_b = exchange(own_a, first_a, devices), exchange(own_b, first_b, devices)
    vmem = pl.BlockSpec(memory_space=pltpu.VMEM)
    smem = pl.BlockSpec(memory_space=pltpu.SMEM)
    ninv = pl.pallas_call(
        functools.partial(energies, masks_a, masks_b, slabs, per),
        out_shape=jax.ShapeDtypeStruct((rows, cols), jnp.float32),
        in_specs=[smem] * 3 + [vmem] * 2,
        compiler_params=pltpu.CompilerParams(vmem_limit_bytes=6 * MIB),
        name="energies",
    )(me.reshape(1), occ_alpha, occ_beta, virt_alpha[:, None], virt_beta.reshape(slabs, block))
    pieces_b, pieces_a, near_a, near_b, ninv = together((pieces_b, pieces_a, near_a, near_b, ninv))
    pieces_a.update(sent_on({1 << first_a: [near_a]}, alpha_bits[1:]))
    pieces_b.update(sent_on({1 << first_b: [near_b]}, beta_bits[1:-1]))
    pieces_b = sent_on(pieces_b, [0])

    def blocks(count):
        return [jax.ShapeDtypeStruct((n, aux), jnp.float32) for n in cut * count]

    def pairs(names, outs):
        return {m: [out] for m, out in zip(names, outs)}

    early_a, early_b = max(n_a // 4, 1), max(n_b // 4, 2)

    def late_first(names, first):
        late = [m for m in names if m & (1 << first) and m & ~(1 << first) & ~1]
        return len(late) if names[:len(late)] == late else len(names)

    late_a, late_b = late_first(masks_a, first_a), late_first(masks_b, first_b)
    corner = (min(-(-late_a * width // 128) * 128, rows), min(-(-late_b * width // 256) * 256, cols))
    all_a = [(v, k * width) for k, m in enumerate(masks_a) for v in pieces_a[m]]
    all_b = [(v, k * width) for k, m in enumerate(masks_b) for v in pieces_b[m]]
    shared = [
        jax.ShapeDtypeStruct((rows, cols), jnp.bfloat16),
        jax.ShapeDtypeStruct((cols, rows), jnp.bfloat16),
        jax.ShapeDtypeStruct((rows, aux), jnp.bfloat16),
        jax.ShapeDtypeStruct((cols, aux), jnp.bfloat16),
    ]

    def estimate(part):
        return pl.CostEstimate(
            flops=2 * part * aux, bytes_accessed=2 * (rows + cols) * aux * 2, transcendentals=0
        )

    begun = pl.pallas_call(
        functools.partial(begin_amplitudes, [p for _, p in all_a[late_a:]], [p for _, p in all_b[late_b:]], corner),
        out_shape=shared + [jax.ShapeDtypeStruct((8, 128), jnp.float32)],
        compiler_params=pltpu.CompilerParams(vmem_limit_bytes=18 * MIB),
        cost_estimate=estimate((rows - corner[0]) * (cols - corner[1])),
        name="amplitudes_early",
    )(*[v for v, _ in all_a[late_a:] + all_b[late_b:]], ninv)
    count = late_a + late_b + 1
    opening = pl.pallas_call(
        functools.partial(
            end_amplitudes, [p for _, p in all_a[:late_a]], [p for _, p in all_b[:late_b]], corner, cut * early_b
        ),
        out_shape=shared + [jax.ShapeDtypeStruct((aux,), jnp.float32)] * 4 + blocks(early_b),
        input_output_aliases={count + k: k for k in range(4)},
        compiler_params=pltpu.CompilerParams(vmem_limit_bytes=24 * MIB),
        cost_estimate=estimate(rows * cols),
        name="amplitudes_late",
    )(*[v for v, _ in all_a[:late_a] + all_b[:late_b]], ninv, *begun)
    t, tt, acat, bcat, scale_a, scale_b, unit_a, unit_b = opening[:8]

    def contracted(left, right, start, names, name):
        outs = pl.pallas_call(
            functools.partial(rows_out, start * width, cut * len(names)),
            out_shape=blocks(len(names)),
            compiler_params=pltpu.CompilerParams(vmem_limit_bytes=14 * MIB),
            cost_estimate=pl.CostEstimate(
                flops=2 * len(names) * width * right.size, bytes_accessed=len(names) * width * aux * 4 + right.size * 2,
                transcendentals=0,
            ),
            name=name,
        )(left, right)
        return pairs(names, outs)

    def narrow(value, scale):
        return (value * scale).astype(jnp.float16)

    def wide(value, unit):
        return value.astype(jnp.float32) * unit

    def passed_on(names, bits, level):
        flag = 1 << bits[level]
        gone = sum(1 << b for b in bits[:level])
        every = [m for m in names if m & flag and not m & gone]
        after = 1 << bits[level + 1] if level + 1 < len(bits) else flag
        ahead = [m for m in every if m & after]
        return ahead, [m for m in every if m not in ahead]

    bits_a, bits_b = alpha_bits[::-1], [b for b in beta_bits[::-1] if b]
    names_b = [m for m in masks_b if not m & 1]
    unit_other = exchange(unit_b, 0, devices)

    def chips_sum(found):
        return {
            m: [v + wide(exchange(narrow(w, scale_b), 0, devices), unit_other) for v, w in zip(vs, found[m | 1])]
            for m, vs in found.items() if not m & 1
        }

    unit_b = unit_b + unit_other
    units, scales = [unit_a, unit_b], [scale_a, 1.0 / unit_b]
    gb = chips_sum(pairs(masks_b, opening[8:]))
    ga = contracted(t, bcat, 0, masks_a[:early_a], "alpha_first")
    for level in range(max(len(bits_a), len(bits_b))):
        jobs = [
            (which, parts, bits[level]) + passed_on(names, bits, level)
            for which, parts, names, bits in ((0, ga, masks_a, bits_a), (1, gb, names_b, bits_b)) if level < len(bits)
        ]

        before = scales

        def made(names_at, by):
            return [[narrow(job[1][m][0], by[job[0]]) for m in job[names_at]] for job in jobs]

        def moved(values):
            return [[exchange(v, job[2], devices) for v in vs] for job, vs in zip(jobs, values)]

        def added(names_at, values):
            for job, vs in zip(jobs, values):
                for m, v in zip(job[names_at], vs):
                    job[1][m ^ (1 << job[2])][0] += wide(v, partner[job[0]])

        if level == 0:
            sent, units, t, tt, acat, bcat = together((made(3, before), units, t, tt, acat, bcat))
            coming = {job[0]: exchange(units[job[0]], job[2], devices) for job in jobs}
        else:
            sent = made(3, before)
        partner = coming
        got = moved(sent)
        if level == 0:
            gb.update(chips_sum(contracted(tt, acat, early_b, masks_b[early_b:], "beta")))
            ga.update(contracted(t, bcat, early_a, masks_a[early_a:], "alpha"))
        units = [units[w] + partner[w] if w in partner else units[w] for w in range(2)]
        scales = [1.0 / unit for unit in units]
        coming = {
            w: exchange(units[w], bits[level + 1], devices)
            for w, bits in ((0, bits_a), (1, bits_b)) if level + 1 < len(bits)
        }
        rest = made(4, before)
        got, rest[0], coming, scales = together((got, rest[0], coming, scales))
        rest = moved(rest)
        added(3, got)
        added(4, rest)

    def whole(parts):
        return parts[0].reshape(orbital_alpha.shape)

    return whole(ga[0]), whole(gb[0])


def solution(mesh):
    in_specs = (P("grp", "slab", None), P("grp", "slab", None), P(), P(), P(), P())
    out_specs = (P("grp", "slab", None), P("grp", "slab", None))
    return jax.shard_map(body, mesh=mesh, in_specs=in_specs, out_specs=out_specs, check_vma=False)
```

```python
import functools

import jax
import jax.numpy as jnp
from jax import lax
from jax.experimental import pallas as pl
from jax.experimental.pallas import tpu as pltpu
from jax.sharding import PartitionSpec as P

MIB = 1024 * 1024
together = lax.optimization_barrier


def bits_of(groups, slabs):
    slab_bits = slabs.bit_length() - 1
    total = (groups * slabs).bit_length() - 1
    shared = min(slab_bits - 1, total // 2)
    alpha = [slab_bits - 1] + list(range(shared - 1, 0, -1))
    beta = list(range(slab_bits - 2, shared - 1, -1)) + list(range(total - 1, slab_bits - 1, -1)) + [0]
    return alpha, beta


def exchange(value, bit, devices):
    return lax.ppermute(value, ("grp", "slab"), [(d, d ^ (1 << bit)) for d in range(devices)])


def energies(masks_a, masks_b, slabs, per, place, occ_a, occ_b, va_ref, vb_ref, ninv):
    width = ninv.shape[0] // len(masks_a)
    me = place[0]
    parts, occs = [], []
    for m in masks_b:
        other = jnp.bitwise_xor(me, m)
        for o in range(per):
            parts.append(vb_ref[pl.ds(other % slabs, 1), :])
            occs.append(jnp.full((1, width // per), occ_b[(other // slabs) * per + o], jnp.float32))
    vb, ob = jnp.concatenate(parts, axis=1), jnp.concatenate(occs, axis=1)
    for p, m in enumerate(masks_a):
        other = jnp.bitwise_xor(me, m)
        at = pl.multiple_of((other % slabs) * (width // per), 8)
        va = jnp.concatenate([va_ref[pl.ds(at, width // per), :]] * per, axis=0)
        oa = jnp.concatenate(
            [jnp.full((width // per, 1), occ_a[(other // slabs) * per + o], jnp.float32) for o in range(per)], axis=0
        )
        ninv[p * width:(p + 1) * width, :] = -1.0 / (((va + vb) - oa) - ob)


def magnitude(value):
    return jnp.max(jnp.max(jnp.abs(value), axis=1, keepdims=True), axis=0, keepdims=True).astype(jnp.float32)


def amplitudes_of(rows, cols, acat, bcat, ninv, t_ref, tt):
    top = jnp.zeros((1, 1), jnp.float32)
    step = 256 if (cols[1] - cols[0]) % 256 == 0 else cols[1] - cols[0]
    for c in range(cols[0], cols[1], step):
        integrals = lax.dot_general(
            acat[rows[0]:rows[1], :], bcat[c:c + step, :], (((1,), (1,)), ((), ())), preferred_element_type=jnp.float32
        )
        amps = integrals * ninv[rows[0]:rows[1], c:c + step]
        top = jnp.maximum(top, magnitude(amps))
        amps = amps.astype(jnp.bfloat16)
        t_ref[rows[0]:rows[1], c:c + step] = amps
        tt[c:c + step, rows[0]:rows[1]] = amps.T
    return top


def joined(sources, places, target):
    top = jnp.zeros((1, 1), jnp.float32)
    for ref, at in zip(sources, places):
        value = ref[...]
        target[at:at + ref.shape[0], :] = value
        top = jnp.maximum(top, magnitude(value))
    return top


def begin_amplitudes(places_a, places_b, corner, *refs):
    n_a, n_b = len(places_a), len(places_b)
    a_refs, b_refs, ninv = refs[:n_a], refs[n_a:n_a + n_b], refs[n_a + n_b]
    t_ref, tt, acat, bcat, tops = refs[n_a + n_b + 1:]
    top_a, top_b = joined(a_refs, places_a, acat), joined(b_refs, places_b, bcat)
    rows, cols = t_ref.shape
    top = jnp.zeros((1, 1), jnp.float32)
    if corner[0] < rows and corner[1] < cols:
        top = amplitudes_of((corner[0], rows), (corner[1], cols), acat, bcat, ninv, t_ref, tt)
    row = lax.broadcasted_iota(jnp.int32, tops.shape, 0)
    tops[...] = jnp.where(row == 0, top, jnp.where(row == 1, top_a, top_b))


def end_amplitudes(places_a, places_b, corner, spans, *refs):
    n_a, n_b = len(places_a), len(places_b)
    a_refs, b_refs, ninv = refs[:n_a], refs[n_a:n_a + n_b], refs[n_a + n_b]
    tops = refs[n_a + n_b + 5]
    t_ref, tt, acat, bcat, scale_a, scale_b, unit_a, unit_b = refs[n_a + n_b + 6:n_a + n_b + 14]
    outs = refs[n_a + n_b + 14:]
    rows, cols = t_ref.shape
    top_a = jnp.maximum(tops[1:2, 0:1], joined(a_refs, places_a, acat))
    top_b = jnp.maximum(tops[2:3, 0:1], joined(b_refs, places_b, bcat))
    top = jnp.maximum(tops[0:1, 0:1], amplitudes_of((0, corner[0]), (0, cols), acat, bcat, ninv, t_ref, tt))
    if corner[0] < rows:
        top = jnp.maximum(top, amplitudes_of((corner[0], rows), (0, corner[1]), acat, bcat, ninv, t_ref, tt))
    for largest_right, count, unit, scale in ((top_b, cols, unit_a, scale_a), (top_a, rows, unit_b, scale_b)):
        value = top * largest_right * (count / 32768.0) + 1e-36
        unit[...] = jnp.broadcast_to(value[0, 0], unit.shape)
        scale[...] = jnp.broadcast_to((1.0 / value)[0, 0], scale.shape)
    rows_out(0, spans, tt, acat, *outs)


def rows_out(start, spans, left, right, *outs):
    aux = right.shape[1]
    tile = 512 if aux % 512 == 0 else 128
    rows = left[start:start + sum(spans), :]

    for at in range(0, aux, tile):
        acc = jnp.dot(rows, right[:, at:at + tile], preferred_element_type=jnp.float32)
        low = 0
        for span, out in zip(spans, outs):
            out[:, at:at + tile] = acc[low:low + span, :]
            low += span


def body(orbital_alpha, orbital_beta, occ_alpha, occ_beta, virt_alpha, virt_beta):
    groups, slabs = lax.axis_size("grp"), lax.axis_size("slab")
    devices = groups * slabs
    me = lax.axis_index("grp") * slabs + lax.axis_index("slab")
    per, block, aux = orbital_alpha.shape
    width = per * block
    own_a, own_b = orbital_alpha.reshape(width, aux), orbital_beta.reshape(width, aux)
    alpha_bits, beta_bits = bits_of(groups, slabs)

    def masks(bits):
        found = [0]
        for bit in bits:
            found = found + [m | (1 << bit) for m in found]
        return found[::-1]

    masks_a, masks_b = masks(alpha_bits), masks([0] + beta_bits[:-1])
    n_a, n_b = len(masks_a), len(masks_b)
    rows, cols = n_a * width, n_b * width

    cut = [width]

    def sent_on(pieces, bits):
        for bit in bits:
            pieces = dict(pieces)
            pieces.update({m | (1 << bit): [exchange(v, bit, devices) for v in vs] for m, vs in list(pieces.items())})
        return pieces

    first_a, first_b = alpha_bits[0], beta_bits[0]
    pieces_a, pieces_b = sent_on({0: [own_a]}, alpha_bits[1:]), sent_on({0: [own_b]}, beta_bits[1:-1])
    near_a, near_b = exchange(own_a, first_a, devices), exchange(own_b, first_b, devices)
    vmem = pl.BlockSpec(memory_space=pltpu.VMEM)
    smem = pl.BlockSpec(memory_space=pltpu.SMEM)
    ninv = pl.pallas_call(
        functools.partial(energies, masks_a, masks_b, slabs, per),
        out_shape=jax.ShapeDtypeStruct((rows, cols), jnp.float32),
        in_specs=[smem] * 3 + [vmem] * 2,
        compiler_params=pltpu.CompilerParams(vmem_limit_bytes=6 * MIB),
        name="energies",
    )(me.reshape(1), occ_alpha, occ_beta, virt_alpha[:, None], virt_beta.reshape(slabs, block))
    beside = exchange(own_b, 0, devices)
    pieces_b, pieces_a, near_a, near_b, beside, ninv = together((pieces_b, pieces_a, near_a, near_b, beside, ninv))
    pieces_a.update(sent_on({1 << first_a: [near_a]}, alpha_bits[1:]))
    pieces_b.update(sent_on({1 << first_b: [near_b]}, beta_bits[1:-1]))
    pieces_b.update({m | 1: [exchange(v, 0, devices) for v in vs] for m, vs in list(pieces_b.items()) if m})
    pieces_b[1] = [beside]

    def blocks(count):
        return [jax.ShapeDtypeStruct((n, aux), jnp.float32) for n in cut * count]

    def pairs(names, outs):
        return {m: [out] for m, out in zip(names, outs)}

    early_a, early_b = max(n_a // 4, 1), max(n_b // 4, 2)

    def late_first(names, first):
        late = [m for m in names if m & (1 << first) and m & ~(1 << first) & ~1]
        return len(late) if names[:len(late)] == late else len(names)

    late_a, late_b = late_first(masks_a, first_a), late_first(masks_b, first_b)
    corner = (min(-(-late_a * width // 128) * 128, rows), min(-(-late_b * width // 256) * 256, cols))
    all_a = [(v, k * width) for k, m in enumerate(masks_a) for v in pieces_a[m]]
    all_b = [(v, k * width) for k, m in enumerate(masks_b) for v in pieces_b[m]]
    shared = [
        jax.ShapeDtypeStruct((rows, cols), jnp.bfloat16),
        jax.ShapeDtypeStruct((cols, rows), jnp.bfloat16),
        jax.ShapeDtypeStruct((rows, aux), jnp.bfloat16),
        jax.ShapeDtypeStruct((cols, aux), jnp.bfloat16),
    ]

    def estimate(part):
        return pl.CostEstimate(
            flops=2 * part * aux, bytes_accessed=2 * (rows + cols) * aux * 2, transcendentals=0
        )

    begun = pl.pallas_call(
        functools.partial(begin_amplitudes, [p for _, p in all_a[late_a:]], [p for _, p in all_b[late_b:]], corner),
        out_shape=shared + [jax.ShapeDtypeStruct((8, 128), jnp.float32)],
        compiler_params=pltpu.CompilerParams(vmem_limit_bytes=18 * MIB),
        cost_estimate=estimate((rows - corner[0]) * (cols - corner[1])),
        name="amplitudes_early",
    )(*[v for v, _ in all_a[late_a:] + all_b[late_b:]], ninv)
    count = late_a + late_b + 1
    opening = pl.pallas_call(
        functools.partial(
            end_amplitudes, [p for _, p in all_a[:late_a]], [p for _, p in all_b[:late_b]], corner, cut * early_b
        ),
        out_shape=shared + [jax.ShapeDtypeStruct((aux,), jnp.float32)] * 4 + blocks(early_b),
        input_output_aliases={count + k: k for k in range(4)},
        compiler_params=pltpu.CompilerParams(vmem_limit_bytes=24 * MIB),
        cost_estimate=estimate(rows * cols),
        name="amplitudes_late",
    )(*[v for v, _ in all_a[:late_a] + all_b[:late_b]], ninv, *begun)
    t, tt, acat, bcat, scale_a, scale_b, unit_a, unit_b = opening[:8]

    def contracted(left, right, start, names, name):
        outs = pl.pallas_call(
            functools.partial(rows_out, start * width, cut * len(names)),
            out_shape=blocks(len(names)),
            compiler_params=pltpu.CompilerParams(vmem_limit_bytes=14 * MIB),
            cost_estimate=pl.CostEstimate(
                flops=2 * len(names) * width * right.size, bytes_accessed=len(names) * width * aux * 4 + right.size * 2,
                transcendentals=0,
            ),
            name=name,
        )(left, right)
        return pairs(names, outs)

    def narrow(value, scale):
        return (value * scale).astype(jnp.float16)

    def wide(value, unit):
        return value.astype(jnp.float32) * unit

    def passed_on(names, bits, level):
        flag = 1 << bits[level]
        gone = sum(1 << b for b in bits[:level])
        every = [m for m in names if m & flag and not m & gone]
        after = 1 << bits[level + 1] if level + 1 < len(bits) else flag
        ahead = [m for m in every if m & after]
        return ahead, [m for m in every if m not in ahead]

    bits_a, bits_b = alpha_bits[::-1], [b for b in beta_bits[::-1] if b]
    names_b = [m for m in masks_b if not m & 1]
    unit_other = exchange(unit_b, 0, devices)

    def chips_sum(found):
        return {
            m: [v + wide(exchange(narrow(w, scale_b), 0, devices), unit_other) for v, w in zip(vs, found[m | 1])]
            for m, vs in found.items() if not m & 1
        }

    unit_b = unit_b + unit_other
    units, scales = [unit_a, unit_b], [scale_a, 1.0 / unit_b]
    gb = chips_sum(pairs(masks_b, opening[8:]))
    ga = contracted(t, bcat, 0, masks_a[:early_a], "alpha_first")
    for level in range(max(len(bits_a), len(bits_b))):
        jobs = [
            (which, parts, bits[level]) + passed_on(names, bits, level)
            for which, parts, names, bits in ((0, ga, masks_a, bits_a), (1, gb, names_b, bits_b)) if level < len(bits)
        ]

        before = scales

        def made(names_at, by):
            return [[narrow(job[1][m][0], by[job[0]]) for m in job[names_at]] for job in jobs]

        def moved(values):
            return [[exchange(v, job[2], devices) for v in vs] for job, vs in zip(jobs, values)]

        def added(names_at, values):
            for job, vs in zip(jobs, values):
                for m, v in zip(job[names_at], vs):
                    job[1][m ^ (1 << job[2])][0] += wide(v, partner[job[0]])

        if level == 0:
            sent, units, t, tt, acat, bcat = together((made(3, before), units, t, tt, acat, bcat))
            coming = {job[0]: exchange(units[job[0]], job[2], devices) for job in jobs}
        else:
            sent = made(3, before)
        partner = coming
        got = moved(sent)
        if level == 0:
            gb.update(chips_sum(contracted(tt, acat, early_b, masks_b[early_b:], "beta")))
            ga.update(contracted(t, bcat, early_a, masks_a[early_a:], "alpha"))
        units = [units[w] + partner[w] if w in partner else units[w] for w in range(2)]
        scales = [1.0 / unit for unit in units]
        coming = {
            w: exchange(units[w], bits[level + 1], devices)
            for w, bits in ((0, bits_a), (1, bits_b)) if level + 1 < len(bits)
        }
        rest = made(4, before)
        got, rest[0], coming, scales = together((got, rest[0], coming, scales))
        rest = moved(rest)
        added(3, got)
        added(4, rest)

    def whole(parts):
        return parts[0].reshape(orbital_alpha.shape)

    return whole(ga[0]), whole(gb[0])


def solution(mesh):
    in_specs = (P("grp", "slab", None), P("grp", "slab", None), P(), P(), P(), P())
    out_specs = (P("grp", "slab", None), P("grp", "slab", None))
    return jax.shard_map(body, mesh=mesh, in_specs=in_specs, out_specs=out_specs, check_vma=False)
```

```python
import functools

import jax
import jax.numpy as jnp
from jax import lax
from jax.experimental import pallas as pl
from jax.experimental.pallas import tpu as pltpu
from jax.sharding import PartitionSpec as P

MIB = 1024 * 1024
together = lax.optimization_barrier


def bits_of(groups, slabs):
    slab_bits = slabs.bit_length() - 1
    total = (groups * slabs).bit_length() - 1
    shared = min(slab_bits - 1, total // 2)
    alpha = [slab_bits - 1] + list(range(shared - 1, 0, -1))
    beta = list(range(slab_bits - 2, shared - 1, -1)) + list(range(total - 1, slab_bits - 1, -1)) + [0]
    return alpha, beta


def exchange(value, bit, devices):
    return lax.ppermute(value, ("grp", "slab"), [(d, d ^ (1 << bit)) for d in range(devices)])


def energies(masks_a, masks_b, slabs, per, place, occ_a, occ_b, va_ref, vb_ref, ninv):
    width = ninv.shape[0] // len(masks_a)
    me = place[0]
    parts, occs = [], []
    for m in masks_b:
        other = jnp.bitwise_xor(me, m)
        for o in range(per):
            parts.append(vb_ref[pl.ds(other % slabs, 1), :])
            occs.append(jnp.full((1, width // per), occ_b[(other // slabs) * per + o], jnp.float32))
    vb, ob = jnp.concatenate(parts, axis=1), jnp.concatenate(occs, axis=1)
    for p, m in enumerate(masks_a):
        other = jnp.bitwise_xor(me, m)
        at = pl.multiple_of((other % slabs) * (width // per), 8)
        va = jnp.concatenate([va_ref[pl.ds(at, width // per), :]] * per, axis=0)
        oa = jnp.concatenate(
            [jnp.full((width // per, 1), occ_a[(other // slabs) * per + o], jnp.float32) for o in range(per)], axis=0
        )
        ninv[p * width:(p + 1) * width, :] = -1.0 / (((va + vb) - oa) - ob)


def magnitude(value):
    return jnp.max(jnp.max(jnp.abs(value), axis=1, keepdims=True), axis=0, keepdims=True).astype(jnp.float32)


def amplitudes_of(rows, cols, acat, bcat, ninv, t_ref, tt):
    top = jnp.zeros((1, 1), jnp.float32)
    step = 256 if (cols[1] - cols[0]) % 256 == 0 else cols[1] - cols[0]
    for c in range(cols[0], cols[1], step):
        integrals = lax.dot_general(
            acat[rows[0]:rows[1], :], bcat[c:c + step, :], (((1,), (1,)), ((), ())), preferred_element_type=jnp.float32
        )
        amps = integrals * ninv[rows[0]:rows[1], c:c + step]
        top = jnp.maximum(top, magnitude(amps))
        amps = amps.astype(jnp.bfloat16)
        t_ref[rows[0]:rows[1], c:c + step] = amps
        tt[c:c + step, rows[0]:rows[1]] = amps.T
    return top


def joined(sources, places, target):
    top = jnp.zeros((1, 1), jnp.float32)
    for ref, at in zip(sources, places):
        value = ref[...]
        target[at:at + ref.shape[0], :] = value
        top = jnp.maximum(top, magnitude(value))
    return top


def begin_amplitudes(places_a, places_b, corner, *refs):
    n_a, n_b = len(places_a), len(places_b)
    a_refs, b_refs, ninv = refs[:n_a], refs[n_a:n_a + n_b], refs[n_a + n_b]
    t_ref, tt, acat, bcat, tops = refs[n_a + n_b + 1:]
    top_a, top_b = joined(a_refs, places_a, acat), joined(b_refs, places_b, bcat)
    rows, cols = t_ref.shape
    top = jnp.zeros((1, 1), jnp.float32)
    if corner[0] < rows and corner[1] < cols:
        top = amplitudes_of((corner[0], rows), (corner[1], cols), acat, bcat, ninv, t_ref, tt)
    row = lax.broadcasted_iota(jnp.int32, tops.shape, 0)
    tops[...] = jnp.where(row == 0, top, jnp.where(row == 1, top_a, top_b))


def end_amplitudes(places_a, places_b, corner, spans, *refs):
    n_a, n_b = len(places_a), len(places_b)
    a_refs, b_refs, ninv = refs[:n_a], refs[n_a:n_a + n_b], refs[n_a + n_b]
    tops = refs[n_a + n_b + 5]
    t_ref, tt, acat, bcat, scale_a, scale_b, unit_a, unit_b = refs[n_a + n_b + 6:n_a + n_b + 14]
    outs = refs[n_a + n_b + 14:]
    rows, cols = t_ref.shape
    top_a = jnp.maximum(tops[1:2, 0:1], joined(a_refs, places_a, acat))
    top_b = jnp.maximum(tops[2:3, 0:1], joined(b_refs, places_b, bcat))
    top = jnp.maximum(tops[0:1, 0:1], amplitudes_of((0, corner[0]), (0, cols), acat, bcat, ninv, t_ref, tt))
    if corner[0] < rows:
        top = jnp.maximum(top, amplitudes_of((corner[0], rows), (0, corner[1]), acat, bcat, ninv, t_ref, tt))
    for largest_right, count, unit, scale in ((top_b, cols, unit_a, scale_a), (top_a, rows, unit_b, scale_b)):
        value = top * largest_right * (count / 32768.0) + 1e-36
        unit[...] = jnp.broadcast_to(value[0, 0], unit.shape)
        scale[...] = jnp.broadcast_to((1.0 / value)[0, 0], scale.shape)
    rows_out(0, spans, tt, acat, *outs)


def rows_out(start, spans, left, right, *outs):
    aux = right.shape[1]
    tile = 512 if aux % 512 == 0 else 128
    rows = left[start:start + sum(spans), :]

    for at in range(0, aux, tile):
        acc = jnp.dot(rows, right[:, at:at + tile], preferred_element_type=jnp.float32)
        low = 0
        for span, out in zip(spans, outs):
            out[:, at:at + tile] = acc[low:low + span, :]
            low += span


def body(orbital_alpha, orbital_beta, occ_alpha, occ_beta, virt_alpha, virt_beta):
    groups, slabs = lax.axis_size("grp"), lax.axis_size("slab")
    devices = groups * slabs
    me = lax.axis_index("grp") * slabs + lax.axis_index("slab")
    per, block, aux = orbital_alpha.shape
    width = per * block
    own_a, own_b = orbital_alpha.reshape(width, aux), orbital_beta.reshape(width, aux)
    alpha_bits, beta_bits = bits_of(groups, slabs)

    def masks(bits):
        found = [0]
        for bit in bits:
            found = found + [m | (1 << bit) for m in found]
        return found[::-1]

    masks_a, masks_b = masks(alpha_bits), masks([0] + beta_bits[:-1])
    n_a, n_b = len(masks_a), len(masks_b)
    rows, cols = n_a * width, n_b * width

    cut = [width]

    def sent_on(pieces, bits):
        for bit in bits:
            pieces = dict(pieces)
            pieces.update({m | (1 << bit): [exchange(v, bit, devices) for v in vs] for m, vs in list(pieces.items())})
        return pieces

    first_a, first_b = alpha_bits[0], beta_bits[0]
    pieces_a, pieces_b = sent_on({0: [own_a]}, alpha_bits[1:]), sent_on({0: [own_b]}, beta_bits[1:-1])
    near_a, near_b = exchange(own_a, first_a, devices), exchange(own_b, first_b, devices)
    vmem = pl.BlockSpec(memory_space=pltpu.VMEM)
    smem = pl.BlockSpec(memory_space=pltpu.SMEM)
    ninv = pl.pallas_call(
        functools.partial(energies, masks_a, masks_b, slabs, per),
        out_shape=jax.ShapeDtypeStruct((rows, cols), jnp.float32),
        in_specs=[smem] * 3 + [vmem] * 2,
        compiler_params=pltpu.CompilerParams(vmem_limit_bytes=6 * MIB),
        name="energies",
    )(me.reshape(1), occ_alpha, occ_beta, virt_alpha[:, None], virt_beta.reshape(slabs, block))
    pieces_b, pieces_a, near_a, near_b, ninv = together((pieces_b, pieces_a, near_a, near_b, ninv))
    pieces_a.update(sent_on({1 << first_a: [near_a]}, alpha_bits[1:]))
    pieces_b.update(sent_on({1 << first_b: [near_b]}, beta_bits[1:-1]))
    pieces_b = sent_on(pieces_b, [0])

    def blocks(count):
        return [jax.ShapeDtypeStruct((n, aux), jnp.float32) for n in cut * count]

    def pairs(names, outs):
        return {m: [out] for m, out in zip(names, outs)}

    early_a, early_b = max(n_a // 4, 1), max(n_b // 4, 2)

    def late_first(names, first):
        late = [m for m in names if m & (1 << first) and m & ~(1 << first) & ~1]
        return len(late) if names[:len(late)] == late else len(names)

    late_a, late_b = late_first(masks_a, first_a), late_first(masks_b, first_b)
    corner = (min(-(-late_a * width // 128) * 128, rows), min(-(-late_b * width // 256) * 256, cols))
    all_a = [(v, k * width) for k, m in enumerate(masks_a) for v in pieces_a[m]]
    all_b = [(v, k * width) for k, m in enumerate(masks_b) for v in pieces_b[m]]
    shared = [
        jax.ShapeDtypeStruct((rows, cols), jnp.bfloat16),
        jax.ShapeDtypeStruct((cols, rows), jnp.bfloat16),
        jax.ShapeDtypeStruct((rows, aux), jnp.bfloat16),
        jax.ShapeDtypeStruct((cols, aux), jnp.bfloat16),
    ]

    def estimate(part):
        return pl.CostEstimate(
            flops=2 * part * aux, bytes_accessed=2 * (rows + cols) * aux * 2, transcendentals=0
        )

    begun = pl.pallas_call(
        functools.partial(begin_amplitudes, [p for _, p in all_a[late_a:]], [p for _, p in all_b[late_b:]], corner),
        out_shape=shared + [jax.ShapeDtypeStruct((8, 128), jnp.float32)],
        compiler_params=pltpu.CompilerParams(vmem_limit_bytes=18 * MIB),
        cost_estimate=estimate((rows - corner[0]) * (cols - corner[1])),
        name="amplitudes_early",
    )(*[v for v, _ in all_a[late_a:] + all_b[late_b:]], ninv)
    count = late_a + late_b + 1
    opening = pl.pallas_call(
        functools.partial(
            end_amplitudes, [p for _, p in all_a[:late_a]], [p for _, p in all_b[:late_b]], corner, cut * early_b
        ),
        out_shape=shared + [jax.ShapeDtypeStruct((aux,), jnp.float32)] * 4 + blocks(early_b),
        input_output_aliases={count + k: k for k in range(4)},
        compiler_params=pltpu.CompilerParams(vmem_limit_bytes=24 * MIB),
        cost_estimate=estimate(rows * cols),
        name="amplitudes_late",
    )(*[v for v, _ in all_a[:late_a] + all_b[:late_b]], ninv, *begun)
    t, tt, acat, bcat, scale_a, scale_b, unit_a, unit_b = opening[:8]

    def contracted(left, right, start, names, name):
        outs = pl.pallas_call(
            functools.partial(rows_out, start * width, cut * len(names)),
            out_shape=blocks(len(names)),
            compiler_params=pltpu.CompilerParams(vmem_limit_bytes=14 * MIB),
            cost_estimate=pl.CostEstimate(
                flops=2 * len(names) * width * right.size, bytes_accessed=len(names) * width * aux * 4 + right.size * 2,
                transcendentals=0,
            ),
            name=name,
        )(left, right)
        return pairs(names, outs)

    def narrow(value, scale):
        return (value * scale).astype(jnp.float16)

    def wide(value, unit):
        return value.astype(jnp.float32) * unit

    def passed_on(names, bits, level):
        flag = 1 << bits[level]
        gone = sum(1 << b for b in bits[:level])
        every = [m for m in names if m & flag and not m & gone]
        after = 1 << bits[level + 1] if level + 1 < len(bits) else flag
        ahead = [m for m in every if m & after]
        return ahead, [m for m in every if m not in ahead]

    bits_a, bits_b = alpha_bits[::-1], [b for b in beta_bits[::-1] if b]
    names_b = [m for m in masks_b if not m & 1]
    unit_other = exchange(unit_b, 0, devices)

    def chips_sum(found):
        return {
            m: [v + wide(exchange(narrow(w, scale_b), 0, devices), unit_other) for v, w in zip(vs, found[m | 1])]
            for m, vs in found.items() if not m & 1
        }

    unit_b = unit_b + unit_other
    units, scales = [unit_a, unit_b], [scale_a, 1.0 / unit_b]
    gb = chips_sum(pairs(masks_b, opening[8:]))
    ga = contracted(t, bcat, 0, masks_a[:early_a], "alpha_first")
    for level in range(max(len(bits_a), len(bits_b))):
        jobs = [
            (which, parts, bits[level]) + passed_on(names, bits, level)
            for which, parts, names, bits in ((0, ga, masks_a, bits_a), (1, gb, names_b, bits_b)) if level < len(bits)
        ]

        before = scales

        def made(names_at, by):
            return [[narrow(job[1][m][0], by[job[0]]) for m in job[names_at]] for job in jobs]

        def moved(values):
            return [[exchange(v, job[2], devices) for v in vs] for job, vs in zip(jobs, values)]

        def added(names_at, values):
            for job, vs in zip(jobs, values):
                for m, v in zip(job[names_at], vs):
                    job[1][m ^ (1 << job[2])][0] += wide(v, partner[job[0]])

        if level == 0:
            sent, units, t, tt, acat, bcat = together((made(3, before), units, t, tt, acat, bcat))
            coming = {job[0]: exchange(units[job[0]], job[2], devices) for job in jobs}
        else:
            sent = made(3, before)
        partner = coming
        got = moved(sent)
        if level == 0:
            gb.update(chips_sum(contracted(tt, acat, early_b, masks_b[early_b:], "beta")))
            ga.update(contracted(t, bcat, early_a, masks_a[early_a:], "alpha"))
        units = [units[w] + partner[w] if w in partner else units[w] for w in range(2)]
        scales = [1.0 / unit for unit in units]
        coming = {
            w: exchange(units[w], bits[level + 1], devices)
            for w, bits in ((0, bits_a), (1, bits_b)) if level + 1 < len(bits)
        }
        rest = made(4, before)
        got, rest[0], coming, scales = together((got, rest[0], coming, scales))
        rest = moved(rest)
        added(3, got)
        added(4, rest)

    def whole(parts):
        return parts[0].reshape(orbital_alpha.shape)

    return whole(ga[0]), whole(gb[0])


def solution(mesh):
    in_specs = (P("grp", "slab", None), P("grp", "slab", None), P(), P(), P(), P())
    out_specs = (P("grp", "slab", None), P("grp", "slab", None))
    return jax.shard_map(body, mesh=mesh, in_specs=in_specs, out_specs=out_specs, check_vma=False)
```

```python
import functools

import jax
import jax.numpy as jnp
from jax import lax
from jax.experimental import pallas as pl
from jax.experimental.pallas import tpu as pltpu
from jax.sharding import PartitionSpec as P

MIB = 1024 * 1024
together = lax.optimization_barrier


def bits_of(groups, slabs):
    slab_bits = slabs.bit_length() - 1
    total = (groups * slabs).bit_length() - 1
    shared = min(slab_bits - 1, total // 2)
    alpha = [slab_bits - 1] + list(range(shared - 1, 0, -1))
    beta = list(range(slab_bits - 2, shared - 1, -1)) + list(range(total - 1, slab_bits - 1, -1)) + [0]
    return alpha, beta


def exchange(value, bit, devices):
    return lax.ppermute(value, ("grp", "slab"), [(d, d ^ (1 << bit)) for d in range(devices)])


def energies(masks_a, masks_b, slabs, per, place, occ_a, occ_b, va_ref, vb_ref, ninv):
    width = ninv.shape[0] // len(masks_a)
    me = place[0]
    parts, occs = [], []
    for m in masks_b:
        other = jnp.bitwise_xor(me, m)
        for o in range(per):
            parts.append(vb_ref[pl.ds(other % slabs, 1), :])
            occs.append(jnp.full((1, width // per), occ_b[(other // slabs) * per + o], jnp.float32))
    vb, ob = jnp.concatenate(parts, axis=1), jnp.concatenate(occs, axis=1)
    for p, m in enumerate(masks_a):
        other = jnp.bitwise_xor(me, m)
        at = pl.multiple_of((other % slabs) * (width // per), 8)
        va = jnp.concatenate([va_ref[pl.ds(at, width // per), :]] * per, axis=0)
        oa = jnp.concatenate(
            [jnp.full((width // per, 1), occ_a[(other // slabs) * per + o], jnp.float32) for o in range(per)], axis=0
        )
        ninv[p * width:(p + 1) * width, :] = -1.0 / (((va + vb) - oa) - ob)


def magnitude(value):
    return jnp.max(jnp.max(jnp.abs(value), axis=1, keepdims=True), axis=0, keepdims=True).astype(jnp.float32)


def amplitudes_of(rows, cols, acat, bcat, ninv, t_ref, tt):
    top = jnp.zeros((1, 1), jnp.float32)
    span = cols[1] - cols[0]
    step = span if span <= 768 or span % 256 else 256
    for c in range(cols[0], cols[1], step):
        integrals = lax.dot_general(
            acat[rows[0]:rows[1], :], bcat[c:c + step, :], (((1,), (1,)), ((), ())), preferred_element_type=jnp.float32
        )
        amps = integrals * ninv[rows[0]:rows[1], c:c + step]
        top = jnp.maximum(top, magnitude(amps))
        amps = amps.astype(jnp.bfloat16)
        t_ref[rows[0]:rows[1], c:c + step] = amps
        tt[c:c + step, rows[0]:rows[1]] = amps.T
    return top


def joined(sources, places, target):
    top = jnp.zeros((1, 1), jnp.float32)
    for ref, at in zip(sources, places):
        value = ref[...]
        target[at:at + ref.shape[0], :] = value
        top = jnp.maximum(top, magnitude(value))
    return top


def begin_amplitudes(places_a, places_b, corner, *refs):
    n_a, n_b = len(places_a), len(places_b)
    a_refs, b_refs, ninv = refs[:n_a], refs[n_a:n_a + n_b], refs[n_a + n_b]
    t_ref, tt, acat, bcat, tops = refs[n_a + n_b + 1:]
    top_a, top_b = joined(a_refs, places_a, acat), joined(b_refs, places_b, bcat)
    rows, cols = t_ref.shape
    top = jnp.zeros((1, 1), jnp.float32)
    if corner[0] < rows and corner[1] < cols:
        top = amplitudes_of((corner[0], rows), (corner[1], cols), acat, bcat, ninv, t_ref, tt)
    row = lax.broadcasted_iota(jnp.int32, tops.shape, 0)
    tops[...] = jnp.where(row == 0, top, jnp.where(row == 1, top_a, top_b))


def end_amplitudes(places_a, places_b, corner, spans, *refs):
    n_a, n_b = len(places_a), len(places_b)
    a_refs, b_refs, ninv = refs[:n_a], refs[n_a:n_a + n_b], refs[n_a + n_b]
    tops = refs[n_a + n_b + 5]
    t_ref, tt, acat, bcat, scale_a, scale_b, unit_a, unit_b = refs[n_a + n_b + 6:n_a + n_b + 14]
    outs = refs[n_a + n_b + 14:]
    rows, cols = t_ref.shape
    top_a = jnp.maximum(tops[1:2, 0:1], joined(a_refs, places_a, acat))
    top_b = jnp.maximum(tops[2:3, 0:1], joined(b_refs, places_b, bcat))
    top = jnp.maximum(tops[0:1, 0:1], amplitudes_of((0, corner[0]), (0, cols), acat, bcat, ninv, t_ref, tt))
    if corner[0] < rows:
        top = jnp.maximum(top, amplitudes_of((corner[0], rows), (0, corner[1]), acat, bcat, ninv, t_ref, tt))
    for largest_right, count, unit, scale in ((top_b, cols, unit_a, scale_a), (top_a, rows, unit_b, scale_b)):
        value = top * largest_right * (count / 32768.0) + 1e-36
        unit[...] = jnp.broadcast_to(value[0, 0], unit.shape)
        scale[...] = jnp.broadcast_to((1.0 / value)[0, 0], scale.shape)
    rows_out(0, spans, tt, acat, *outs)


def rows_out(start, spans, left, right, *outs):
    aux = right.shape[1]
    tile = 1280 if aux % 1280 == 0 else 128
    rows = left[start:start + sum(spans), :]

    for at in range(0, aux, tile):
        acc = jnp.dot(rows, right[:, at:at + tile], preferred_element_type=jnp.float32)
        low = 0
        for span, out in zip(spans, outs):
            out[:, at:at + tile] = acc[low:low + span, :]
            low += span


def body(orbital_alpha, orbital_beta, occ_alpha, occ_beta, virt_alpha, virt_beta):
    groups, slabs = lax.axis_size("grp"), lax.axis_size("slab")
    devices = groups * slabs
    me = lax.axis_index("grp") * slabs + lax.axis_index("slab")
    per, block, aux = orbital_alpha.shape
    width = per * block
    own_a, own_b = orbital_alpha.reshape(width, aux), orbital_beta.reshape(width, aux)
    alpha_bits, beta_bits = bits_of(groups, slabs)

    def masks(bits):
        found = [0]
        for bit in bits:
            found = found + [m | (1 << bit) for m in found]
        return found[::-1]

    masks_a, masks_b = masks(alpha_bits), masks([0] + beta_bits[:-1])
    n_a, n_b = len(masks_a), len(masks_b)
    rows, cols = n_a * width, n_b * width

    cut = [width]

    def sent_on(pieces, bits):
        for bit in bits:
            pieces = dict(pieces)
            pieces.update({m | (1 << bit): [exchange(v, bit, devices) for v in vs] for m, vs in list(pieces.items())})
        return pieces

    first_a, first_b = alpha_bits[0], beta_bits[0]
    pieces_a, pieces_b = sent_on({0: [own_a]}, alpha_bits[1:]), sent_on({0: [own_b]}, beta_bits[1:-1])
    near_a, near_b = exchange(own_a, first_a, devices), exchange(own_b, first_b, devices)
    vmem = pl.BlockSpec(memory_space=pltpu.VMEM)
    smem = pl.BlockSpec(memory_space=pltpu.SMEM)
    ninv = pl.pallas_call(
        functools.partial(energies, masks_a, masks_b, slabs, per),
        out_shape=jax.ShapeDtypeStruct((rows, cols), jnp.float32),
        in_specs=[smem] * 3 + [vmem] * 2,
        compiler_params=pltpu.CompilerParams(vmem_limit_bytes=6 * MIB),
        name="energies",
    )(me.reshape(1), occ_alpha, occ_beta, virt_alpha[:, None], virt_beta.reshape(slabs, block))
    pieces_b, pieces_a, near_a, near_b, ninv = together((pieces_b, pieces_a, near_a, near_b, ninv))
    pieces_a.update(sent_on({1 << first_a: [near_a]}, alpha_bits[1:]))
    pieces_b.update(sent_on({1 << first_b: [near_b]}, beta_bits[1:-1]))
    pieces_b = sent_on(pieces_b, [0])

    def blocks(count):
        return [jax.ShapeDtypeStruct((n, aux), jnp.float32) for n in cut * count]

    def pairs(names, outs):
        return {m: [out] for m, out in zip(names, outs)}

    early_a, early_b = max(n_a // 4, 1), max(n_b // 4, 2)

    def late_first(names, first):
        late = [m for m in names if m & (1 << first) and m & ~(1 << first) & ~1]
        return len(late) if names[:len(late)] == late else len(names)

    late_a, late_b = late_first(masks_a, first_a), late_first(masks_b, first_b)
    corner = (min(-(-late_a * width // 128) * 128, rows), min(-(-late_b * width // 256) * 256, cols))
    all_a = [(v, k * width) for k, m in enumerate(masks_a) for v in pieces_a[m]]
    all_b = [(v, k * width) for k, m in enumerate(masks_b) for v in pieces_b[m]]
    shared = [
        jax.ShapeDtypeStruct((rows, cols), jnp.bfloat16),
        jax.ShapeDtypeStruct((cols, rows), jnp.bfloat16),
        jax.ShapeDtypeStruct((rows, aux), jnp.bfloat16),
        jax.ShapeDtypeStruct((cols, aux), jnp.bfloat16),
    ]

    def estimate(part):
        return pl.CostEstimate(
            flops=2 * part * aux, bytes_accessed=2 * (rows + cols) * aux * 2, transcendentals=0
        )

    begun = pl.pallas_call(
        functools.partial(begin_amplitudes, [p for _, p in all_a[late_a:]], [p for _, p in all_b[late_b:]], corner),
        out_shape=shared + [jax.ShapeDtypeStruct((8, 128), jnp.float32)],
        compiler_params=pltpu.CompilerParams(vmem_limit_bytes=18 * MIB),
        cost_estimate=estimate((rows - corner[0]) * (cols - corner[1])),
        name="amplitudes_early",
    )(*[v for v, _ in all_a[late_a:] + all_b[late_b:]], ninv)
    count = late_a + late_b + 1
    opening = pl.pallas_call(
        functools.partial(
            end_amplitudes, [p for _, p in all_a[:late_a]], [p for _, p in all_b[:late_b]], corner, cut * early_b
        ),
        out_shape=shared + [jax.ShapeDtypeStruct((aux,), jnp.float32)] * 4 + blocks(early_b),
        input_output_aliases={count + k: k for k in range(4)},
        compiler_params=pltpu.CompilerParams(vmem_limit_bytes=24 * MIB),
        cost_estimate=estimate(rows * cols),
        name="amplitudes_late",
    )(*[v for v, _ in all_a[:late_a] + all_b[:late_b]], ninv, *begun)
    t, tt, acat, bcat, scale_a, scale_b, unit_a, unit_b = opening[:8]

    def contracted(left, right, start, names, name):
        outs = pl.pallas_call(
            functools.partial(rows_out, start * width, cut * len(names)),
            out_shape=blocks(len(names)),
            compiler_params=pltpu.CompilerParams(vmem_limit_bytes=14 * MIB),
            cost_estimate=pl.CostEstimate(
                flops=2 * len(names) * width * right.size, bytes_accessed=len(names) * width * aux * 4 + right.size * 2,
                transcendentals=0,
            ),
            name=name,
        )(left, right)
        return pairs(names, outs)

    def narrow(value, scale):
        return (value * scale).astype(jnp.float16)

    def wide(value, unit):
        return value.astype(jnp.float32) * unit

    def passed_on(names, bits, level):
        flag = 1 << bits[level]
        gone = sum(1 << b for b in bits[:level])
        every = [m for m in names if m & flag and not m & gone]
        after = 1 << bits[level + 1] if level + 1 < len(bits) else flag
        ahead = [m for m in every if m & after]
        return ahead, [m for m in every if m not in ahead]

    bits_a, bits_b = alpha_bits[::-1], [b for b in beta_bits[::-1] if b]
    names_b = [m for m in masks_b if not m & 1]
    unit_other = exchange(unit_b, 0, devices)

    def chips_sum(found):
        return {
            m: [v + wide(exchange(narrow(w, scale_b), 0, devices), unit_other) for v, w in zip(vs, found[m | 1])]
            for m, vs in found.items() if not m & 1
        }

    unit_b = unit_b + unit_other
    units, scales = [unit_a, unit_b], [scale_a, 1.0 / unit_b]
    gb = chips_sum(pairs(masks_b, opening[8:]))
    ga = contracted(t, bcat, 0, masks_a[:early_a], "alpha_first")
    for level in range(max(len(bits_a), len(bits_b))):
        jobs = [
            (which, parts, bits[level]) + passed_on(names, bits, level)
            for which, parts, names, bits in ((0, ga, masks_a, bits_a), (1, gb, names_b, bits_b)) if level < len(bits)
        ]

        before = scales

        def made(names_at, by):
            return [[narrow(job[1][m][0], by[job[0]]) for m in job[names_at]] for job in jobs]

        def moved(values):
            return [[exchange(v, job[2], devices) for v in vs] for job, vs in zip(jobs, values)]

        def added(names_at, values):
            for job, vs in zip(jobs, values):
                for m, v in zip(job[names_at], vs):
                    job[1][m ^ (1 << job[2])][0] += wide(v, partner[job[0]])

        if level == 0:
            sent, units, t, tt, acat, bcat = together((made(3, before), units, t, tt, acat, bcat))
            coming = {job[0]: exchange(units[job[0]], job[2], devices) for job in jobs}
        else:
            sent = made(3, before)
        partner = coming
        got = moved(sent)
        if level == 0:
            gb.update(chips_sum(contracted(tt, acat, early_b, masks_b[early_b:], "beta")))
            ga.update(contracted(t, bcat, early_a, masks_a[early_a:], "alpha"))
        units = [units[w] + partner[w] if w in partner else units[w] for w in range(2)]
        scales = [1.0 / unit for unit in units]
        coming = {
            w: exchange(units[w], bits[level + 1], devices)
            for w, bits in ((0, bits_a), (1, bits_b)) if level + 1 < len(bits)
        }
        rest = made(4, before)
        got, rest[0], coming, scales = together((got, rest[0], coming, scales))
        rest = moved(rest)
        added(3, got)
        added(4, rest)

    def whole(parts):
        return parts[0].reshape(orbital_alpha.shape)

    return whole(ga[0]), whole(gb[0])


def solution(mesh):
    in_specs = (P("grp", "slab", None), P("grp", "slab", None), P(), P(), P(), P())
    out_specs = (P("grp", "slab", None), P("grp", "slab", None))
    return jax.shard_map(body, mesh=mesh, in_specs=in_specs, out_specs=out_specs, check_vma=False)
```

```python
import functools

import jax
import jax.numpy as jnp
from jax import lax
from jax.experimental import pallas as pl
from jax.experimental.pallas import tpu as pltpu
from jax.sharding import PartitionSpec as P

MIB = 1024 * 1024
together = lax.optimization_barrier


def bits_of(groups, slabs):
    slab_bits = slabs.bit_length() - 1
    total = (groups * slabs).bit_length() - 1
    shared = min(slab_bits - 1, total // 2)
    alpha = [slab_bits - 1] + list(range(shared - 1, 0, -1))
    beta = list(range(slab_bits - 2, shared - 1, -1)) + list(range(total - 1, slab_bits - 1, -1)) + [0]
    return alpha, beta


def exchange(value, bit, devices):
    return lax.ppermute(value, ("grp", "slab"), [(d, d ^ (1 << bit)) for d in range(devices)])


def energies(masks_a, masks_b, slabs, per, place, occ_a, occ_b, va_ref, vb_ref, ninv):
    width = ninv.shape[0] // len(masks_a)
    me = place[0]
    parts, occs = [], []
    for m in masks_b:
        other = jnp.bitwise_xor(me, m)
        for o in range(per):
            parts.append(vb_ref[pl.ds(other % slabs, 1), :])
            occs.append(jnp.full((1, width // per), occ_b[(other // slabs) * per + o], jnp.float32))
    vb, ob = jnp.concatenate(parts, axis=1), jnp.concatenate(occs, axis=1)
    for p, m in enumerate(masks_a):
        other = jnp.bitwise_xor(me, m)
        at = pl.multiple_of((other % slabs) * (width // per), 8)
        va = jnp.concatenate([va_ref[pl.ds(at, width // per), :]] * per, axis=0)
        oa = jnp.concatenate(
            [jnp.full((width // per, 1), occ_a[(other // slabs) * per + o], jnp.float32) for o in range(per)], axis=0
        )
        ninv[p * width:(p + 1) * width, :] = -1.0 / (((va + vb) - oa) - ob)


def magnitude(value):
    return jnp.max(jnp.max(jnp.abs(value), axis=1, keepdims=True), axis=0, keepdims=True).astype(jnp.float32)


def amplitudes_of(rows, cols, acat, bcat, ninv, t_ref, tt):
    top = jnp.zeros((1, 1), jnp.float32)
    span = cols[1] - cols[0]
    step = span if span <= 768 or span % 256 else 256
    for c in range(cols[0], cols[1], step):
        integrals = lax.dot_general(
            acat[rows[0]:rows[1], :], bcat[c:c + step, :], (((1,), (1,)), ((), ())), preferred_element_type=jnp.float32
        )
        amps = integrals * ninv[rows[0]:rows[1], c:c + step]
        top = jnp.maximum(top, magnitude(amps))
        amps = amps.astype(jnp.bfloat16)
        t_ref[rows[0]:rows[1], c:c + step] = amps
        tt[c:c + step, rows[0]:rows[1]] = amps.T
    return top


def joined(sources, places, target):
    top = jnp.zeros((1, 1), jnp.float32)
    for ref, at in zip(sources, places):
        value = ref[...]
        target[at:at + ref.shape[0], :] = value
        top = jnp.maximum(top, magnitude(value))
    return top


def begin_amplitudes(places_a, places_b, corner, *refs):
    n_a, n_b = len(places_a), len(places_b)
    a_refs, b_refs, ninv = refs[:n_a], refs[n_a:n_a + n_b], refs[n_a + n_b]
    t_ref, tt, acat, bcat, tops = refs[n_a + n_b + 1:]
    top_a, top_b = joined(a_refs, places_a, acat), joined(b_refs, places_b, bcat)
    rows, cols = t_ref.shape
    top = jnp.zeros((1, 1), jnp.float32)
    if corner[0] < rows and corner[1] < cols:
        top = amplitudes_of((corner[0], rows), (corner[1], cols), acat, bcat, ninv, t_ref, tt)
    row = lax.broadcasted_iota(jnp.int32, tops.shape, 0)
    tops[...] = jnp.where(row == 0, top, jnp.where(row == 1, top_a, top_b))


def end_amplitudes(places_a, places_b, corner, spans, *refs):
    n_a, n_b = len(places_a), len(places_b)
    a_refs, b_refs, ninv = refs[:n_a], refs[n_a:n_a + n_b], refs[n_a + n_b]
    tops = refs[n_a + n_b + 5]
    t_ref, tt, acat, bcat, scale_a, scale_b, unit_a, unit_b = refs[n_a + n_b + 6:n_a + n_b + 14]
    outs = refs[n_a + n_b + 14:]
    rows, cols = t_ref.shape
    top_a = jnp.maximum(tops[1:2, 0:1], joined(a_refs, places_a, acat))
    top_b = jnp.maximum(tops[2:3, 0:1], joined(b_refs, places_b, bcat))
    top = jnp.maximum(tops[0:1, 0:1], amplitudes_of((0, corner[0]), (0, cols), acat, bcat, ninv, t_ref, tt))
    if corner[0] < rows:
        top = jnp.maximum(top, amplitudes_of((corner[0], rows), (0, corner[1]), acat, bcat, ninv, t_ref, tt))
    for largest_right, count, unit, scale in ((top_b, cols, unit_a, scale_a), (top_a, rows, unit_b, scale_b)):
        value = top * largest_right * (count / 32768.0) + 1e-36
        unit[...] = jnp.broadcast_to(value[0, 0], unit.shape)
        scale[...] = jnp.broadcast_to((1.0 / value)[0, 0], scale.shape)
    rows_out(0, spans, tt, acat, *outs)


def rows_out(start, spans, left, right, *outs):
    aux = right.shape[1]
    tile = 1280 if aux % 1280 == 0 else 128
    rows = left[start:start + sum(spans), :]

    for at in range(0, aux, tile):
        acc = jnp.dot(rows, right[:, at:at + tile], preferred_element_type=jnp.float32)
        low = 0
        for span, out in zip(spans, outs):
            out[:, at:at + tile] = acc[low:low + span, :]
            low += span


def body(orbital_alpha, orbital_beta, occ_alpha, occ_beta, virt_alpha, virt_beta):
    groups, slabs = lax.axis_size("grp"), lax.axis_size("slab")
    devices = groups * slabs
    me = lax.axis_index("grp") * slabs + lax.axis_index("slab")
    per, block, aux = orbital_alpha.shape
    width = per * block
    own_a, own_b = orbital_alpha.reshape(width, aux), orbital_beta.reshape(width, aux)
    alpha_bits, beta_bits = bits_of(groups, slabs)

    def masks(bits):
        found = [0]
        for bit in bits:
            found = found + [m | (1 << bit) for m in found]
        return found[::-1]

    masks_a, masks_b = masks(alpha_bits), masks([0] + beta_bits[:-1])
    n_a, n_b = len(masks_a), len(masks_b)
    rows, cols = n_a * width, n_b * width

    cut = [width]

    def sent_on(pieces, bits):
        for bit in bits:
            pieces = dict(pieces)
            pieces.update({m | (1 << bit): [exchange(v, bit, devices) for v in vs] for m, vs in list(pieces.items())})
        return pieces

    first_a, first_b = alpha_bits[0], beta_bits[0]
    pieces_a, pieces_b = sent_on({0: [own_a]}, alpha_bits[1:]), sent_on({0: [own_b]}, beta_bits[1:-1])
    near_a, near_b = exchange(own_a, first_a, devices), exchange(own_b, first_b, devices)
    vmem = pl.BlockSpec(memory_space=pltpu.VMEM)
    smem = pl.BlockSpec(memory_space=pltpu.SMEM)
    ninv = pl.pallas_call(
        functools.partial(energies, masks_a, masks_b, slabs, per),
        out_shape=jax.ShapeDtypeStruct((rows, cols), jnp.float32),
        in_specs=[smem] * 3 + [vmem] * 2,
        compiler_params=pltpu.CompilerParams(vmem_limit_bytes=6 * MIB),
        name="energies",
    )(me.reshape(1), occ_alpha, occ_beta, virt_alpha[:, None], virt_beta.reshape(slabs, block))
    pieces_b, pieces_a, near_a, near_b, ninv = together((pieces_b, pieces_a, near_a, near_b, ninv))
    pieces_a.update(sent_on({1 << first_a: [near_a]}, alpha_bits[1:]))
    pieces_b.update(sent_on({1 << first_b: [near_b]}, beta_bits[1:-1]))
    pieces_b = sent_on(pieces_b, [0])

    def blocks(count):
        return [jax.ShapeDtypeStruct((n, aux), jnp.float32) for n in cut * count]

    def pairs(names, outs):
        return {m: [out] for m, out in zip(names, outs)}

    early_a, early_b = max(n_a // 4, 1), max(n_b // 4, 2)
    ahead_b = 1 if early_b == 2 else early_b

    def late_first(names, first):
        late = [m for m in names if m & (1 << first) and m & ~(1 << first) & ~1]
        return len(late) if names[:len(late)] == late else len(names)

    late_a, late_b = late_first(masks_a, first_a), late_first(masks_b, first_b)
    corner = (min(-(-late_a * width // 128) * 128, rows), min(-(-late_b * width // 256) * 256, cols))
    all_a = [(v, k * width) for k, m in enumerate(masks_a) for v in pieces_a[m]]
    all_b = [(v, k * width) for k, m in enumerate(masks_b) for v in pieces_b[m]]
    shared = [
        jax.ShapeDtypeStruct((rows, cols), jnp.bfloat16),
        jax.ShapeDtypeStruct((cols, rows), jnp.bfloat16),
        jax.ShapeDtypeStruct((rows, aux), jnp.bfloat16),
        jax.ShapeDtypeStruct((cols, aux), jnp.bfloat16),
    ]

    def estimate(part):
        return pl.CostEstimate(
            flops=2 * part * aux, bytes_accessed=2 * (rows + cols) * aux * 2, transcendentals=0
        )

    begun = pl.pallas_call(
        functools.partial(begin_amplitudes, [p for _, p in all_a[late_a:]], [p for _, p in all_b[late_b:]], corner),
        out_shape=shared + [jax.ShapeDtypeStruct((8, 128), jnp.float32)],
        compiler_params=pltpu.CompilerParams(vmem_limit_bytes=18 * MIB),
        cost_estimate=estimate((rows - corner[0]) * (cols - corner[1])),
        name="amplitudes_early",
    )(*[v for v, _ in all_a[late_a:] + all_b[late_b:]], ninv)
    count = late_a + late_b + 1
    opening = pl.pallas_call(
        functools.partial(
            end_amplitudes, [p for _, p in all_a[:late_a]], [p for _, p in all_b[:late_b]], corner, cut * ahead_b
        ),
        out_shape=shared + [jax.ShapeDtypeStruct((aux,), jnp.float32)] * 4 + blocks(ahead_b),
        input_output_aliases={count + k: k for k in range(4)},
        compiler_params=pltpu.CompilerParams(vmem_limit_bytes=24 * MIB),
        cost_estimate=estimate(rows * cols),
        name="amplitudes_late",
    )(*[v for v, _ in all_a[:late_a] + all_b[:late_b]], ninv, *begun)
    t, tt, acat, bcat, scale_a, scale_b, unit_a, unit_b = opening[:8]

    def contracted(left, right, start, names, name):
        outs = pl.pallas_call(
            functools.partial(rows_out, start * width, cut * len(names)),
            out_shape=blocks(len(names)),
            compiler_params=pltpu.CompilerParams(vmem_limit_bytes=14 * MIB),
            cost_estimate=pl.CostEstimate(
                flops=2 * len(names) * width * right.size, bytes_accessed=len(names) * width * aux * 4 + right.size * 2,
                transcendentals=0,
            ),
            name=name,
        )(left, right)
        return pairs(names, outs)

    def narrow(value, scale):
        return (value * scale).astype(jnp.float16)

    def wide(value, unit):
        return value.astype(jnp.float32) * unit

    def passed_on(names, bits, level):
        flag = 1 << bits[level]
        gone = sum(1 << b for b in bits[:level])
        every = [m for m in names if m & flag and not m & gone]
        after = 1 << bits[level + 1] if level + 1 < len(bits) else flag
        ahead = [m for m in every if m & after]
        return ahead, [m for m in every if m not in ahead]

    bits_a, bits_b = alpha_bits[::-1], [b for b in beta_bits[::-1] if b]
    names_b = [m for m in masks_b if not m & 1]
    unit_other = exchange(unit_b, 0, devices)

    def chips_sum(found):
        return {
            m: [v + wide(exchange(narrow(w, scale_b), 0, devices), unit_other) for v, w in zip(vs, found[m | 1])]
            for m, vs in found.items() if not m & 1
        }

    unit_b = unit_b + unit_other
    units, scales = [unit_a, unit_b], [scale_a, 1.0 / unit_b]
    gb = pairs(masks_b, opening[8:])
    if ahead_b < early_b:
        gb.update(contracted(tt, acat, ahead_b, masks_b[ahead_b:early_b], "beta_first"))
    gb = chips_sum(gb)
    ga = contracted(t, bcat, 0, masks_a[:early_a], "alpha_first")
    for level in range(max(len(bits_a), len(bits_b))):
        jobs = [
            (which, parts, bits[level]) + passed_on(names, bits, level)
            for which, parts, names, bits in ((0, ga, masks_a, bits_a), (1, gb, names_b, bits_b)) if level < len(bits)
        ]

        before = scales

        def made(names_at, by):
            return [[narrow(job[1][m][0], by[job[0]]) for m in job[names_at]] for job in jobs]

        def moved(values):
            return [[exchange(v, job[2], devices) for v in vs] for job, vs in zip(jobs, values)]

        def added(names_at, values):
            for job, vs in zip(jobs, values):
                for m, v in zip(job[names_at], vs):
                    job[1][m ^ (1 << job[2])][0] += wide(v, partner[job[0]])

        if level == 0:
            sent, units, t, tt, acat, bcat = together((made(3, before), units, t, tt, acat, bcat))
            coming = {job[0]: exchange(units[job[0]], job[2], devices) for job in jobs}
        else:
            sent = made(3, before)
        partner = coming
        got = moved(sent)
        if level == 0:
            gb.update(chips_sum(contracted(tt, acat, early_b, masks_b[early_b:], "beta")))
            ga.update(contracted(t, bcat, early_a, masks_a[early_a:], "alpha"))
        units = [units[w] + partner[w] if w in partner else units[w] for w in range(2)]
        scales = [1.0 / unit for unit in units]
        coming = {
            w: exchange(units[w], bits[level + 1], devices)
            for w, bits in ((0, bits_a), (1, bits_b)) if level + 1 < len(bits)
        }
        rest = made(4, before)
        got, rest[0], coming, scales = together((got, rest[0], coming, scales))
        rest = moved(rest)
        added(3, got)
        added(4, rest)

    def whole(parts):
        return parts[0].reshape(orbital_alpha.shape)

    return whole(ga[0]), whole(gb[0])


def solution(mesh):
    in_specs = (P("grp", "slab", None), P("grp", "slab", None), P(), P(), P(), P())
    out_specs = (P("grp", "slab", None), P("grp", "slab", None))
    return jax.shard_map(body, mesh=mesh, in_specs=in_specs, out_specs=out_specs, check_vma=False)
```
